512 devices in a mesh: dp: 128 (over z, y_lo, x, core), tensor: 4 (over y_hi).
Axes of the slice: x: 4, y: 8 (y_hi: 4, y_lo: 2; y = y_hi * 2 + y_lo), z: 8, core: 2. Of those that a mesh axis runs over, the one named last changes fastest.
Arguments:
- activations: bfloat16 [65536, 4096], P('dp', 'tensor'), may hold values from -512 to 512
- token_mask: int32 [65536], P('dp'), may hold values 0 or 1
- gradient: bfloat16 [16384, 4096], P(('dp', 'tensor')), may hold values from -6 to 6
Outputs:
- preconditioned: bfloat16 [16384, 4096], P(('dp', 'tensor'))
The draws below stay inside these ranges and needn't reach their ends.
All inputs are finite; a program needn't handle non-finite values. Where the reference program divides by a largest or mean magnitude, that divisor is 1e-20 or more. No bound on the sum of `token_mask` on one device may be relied on, other than what follows from the above.
Results may differ from the reference program's by a relative error of at most 0.0049.
Values may be sent and summed in bfloat16 or wider, within the bound.
No kernel may reach another device: no remote copies, remote signals or barrier semaphores. Data moves between devices by JAX's collectives and lax.ppermute only.
A program may use at most 64 MiB of HBM per device.

```python
import jax
import jax.numpy as jnp
from jax import lax

B = 512
NS_ITERS = 3
TOK_DEV = 512
NBLK = 8
FEAT = 4096
TOKENS = 65536
QCOLS = 16384


def draw_activations(key, part):
    key = jax.random.fold_in(key, 11)
    noise_key, scale_key, perm_key = jax.random.split(key, 3)
    noise_draw = jax.random.normal(noise_key, (TOKENS, FEAT), jnp.float32)
    mixed_rows = noise_draw + 0.8 * jnp.roll(noise_draw, -1, axis=1)
    col_scale = jnp.exp(jax.random.uniform(scale_key, (1, FEAT), jnp.float32, 0.0, 1.15))
    device_count = TOKENS // TOK_DEV
    band_width = FEAT // device_count
    chosen = jax.random.permutation(perm_key, device_count)
    row_band = chosen[jnp.arange(TOKENS) // TOK_DEV]
    col_band = jnp.arange(FEAT) // band_width
    boost_factor = jnp.where(row_band[:, None] == col_band[None, :], 6.0, 1.0)
    return (mixed_rows * col_scale * boost_factor).astype(jnp.bfloat16)


def touch_ends(array, own_key, low, top_value):
    dims = array.shape
    spot = [jax.random.randint(jax.random.fold_in(own_key, axis), (), 0, dims[axis]) for axis in range(len(dims))]
    array = array.at[tuple(spot)].set(low)
    longest = dims.index(max(dims))
    spot[longest] = (spot[longest] + 1) % dims[longest]
    return array.at[tuple(spot)].set(top_value)


def steps_of(own_key, shape, cuts, low, high):
    def one(dim, blocks):
        draws = jax.random.uniform(jax.random.fold_in(jax.random.fold_in(own_key, 6), dim), (blocks,), jnp.float32, low / len(cuts), high / len(cuts))
        return jnp.repeat(jnp.exp(draws), shape[dim] // blocks).reshape((-1,) + (1,) * (len(shape) - dim - 1))

    factor_of = one(*cuts[0])
    for cut in cuts[1:]:
        factor_of = factor_of * one(*cut)
    return factor_of


def noise(rng, dims, deviation, reach, cuts=(), kind=jnp.bfloat16):
    drawn = deviation * jax.random.normal(rng, dims, jnp.float32)
    if cuts:
        drawn = drawn * steps_of(rng, dims, cuts, -0.22, 0.18)
    return jnp.clip(drawn, -reach, reach).astype(kind)


def setup_inputs(seed: int = 0) -> dict:
    key_list = jax.random.split(jax.random.key(seed), 4)
    activations = draw_activations(jax.random.fold_in(key_list[3], 71), 0)
    token_mask = touch_ends((jax.random.randint(key_list[1], (TOKENS,), 0, 4) < 3).astype(jnp.int32), jax.random.fold_in(key_list[1], 1), 0, 1)
    gradient = noise(key_list[2], (QCOLS, FEAT), 1.0, 6.0, ((0, 512),))
    return {"activations": activations, "token_mask": token_mask, "gradient": gradient}


DAMPING = 0.05

def inverse_root(gram_block):
    identity = jnp.eye(gram_block.shape[0], dtype=jnp.float32)
    damped = gram_block / TOKENS + DAMPING * identity
    scale_norm = jnp.max(lax.optimization_barrier(jnp.sum(jnp.abs(damped), axis=1)))
    iterate = damped / scale_norm
    inverse = identity
    for sweep_index in range(NS_ITERS):
        middle = 1.5 * identity - 0.5 * jnp.dot(inverse, iterate, precision=lax.Precision.HIGHEST)
        if sweep_index + 1 < NS_ITERS:
            iterate = jnp.dot(iterate, middle, precision=lax.Precision.HIGHEST)
        inverse = jnp.dot(middle, inverse, precision=lax.Precision.HIGHEST)
    return (inverse / jnp.sqrt(scale_norm)).astype(jnp.bfloat16)

def reference(activations, token_mask, gradient):
    masked = activations * token_mask.astype(jnp.bfloat16)[:, None]
    results = []
    for block_index in range(NBLK):
        block_cols = masked[:, block_index * B:(block_index + 1) * B]
        gram_block = jnp.dot(block_cols.T, block_cols, preferred_element_type=jnp.float32)
        root_block = inverse_root(gram_block)
        grad_cols = gradient[:, block_index * B:(block_index + 1) * B]
        results.append(jnp.dot(grad_cols, root_block, preferred_element_type=jnp.float32).astype(jnp.bfloat16))
    return jnp.concatenate(results, axis=1)
```

```python
import jax
import jax.numpy as jnp
from jax import lax
from jax.experimental import pallas as pl
from jax.experimental.pallas import tpu as pltpu
from jax.sharding import Mesh, PartitionSpec as P

B = 512
H = 256
LANES = 128
DAMPING = 0.05
BF = jnp.bfloat16
F32 = jnp.float32
AXES = (("z", 4), ("yl", 2), ("x", 8), ("core", 2), ("yh", 4))
SHARDS = 8
PACKED = 3 * 2 * H // SHARDS
VMEM = pl.BlockSpec(memory_space=pltpu.VMEM)


def call(kernel, out, *operands):
    return pl.pallas_call(
        kernel,
        out_shape=jax.ShapeDtypeStruct(*out),
        in_specs=[VMEM] * len(operands),
        out_specs=VMEM,
        compiler_params=pltpu.CompilerParams(vmem_limit_bytes=40 * 1024 * 1024),
    )(*operands)


def tdot(left, right):
    return lax.dot_general(left, right, (((0,), (0,)), ((), ())), preferred_element_type=F32)


def gram_kernel(own_ref, other_ref, out_ref):
    lows, highs = [], []
    for ref in (own_ref, other_ref):
        lows.append(ref[:, :H])
        highs.append(ref[:, H:])
    for slot, (left, right) in enumerate(((lows, lows), (highs, lows), (highs, highs))):
        block = tdot(left[0], right[0]) + tdot(left[1], right[1])
        for half in range(2):
            out_ref[2 * slot + half] = block[:, half * LANES : (half + 1) * LANES].astype(BF)


def sum_kernel(parts_ref, out_ref):
    total = parts_ref[0].astype(F32)
    for part in range(1, SHARDS):
        total += parts_ref[part].astype(F32)
    rounded = total.astype(BF)
    for copy in range(SHARDS):
        out_ref[copy] = rounded


def split(array):
    high = array.astype(BF)
    return high, (array - high.astype(F32)).astype(BF)


def dot3(left, right):
    one = lambda a, b: jnp.dot(a, b, preferred_element_type=F32)
    return one(left[0], right[0]) + (one(left[0], right[1]) + one(left[1], right[0]))


def root_kernel(gram_ref, rows_ref, out_ref):
    packed = [gram_ref[piece].astype(F32) for piece in range(6)]
    first, cross, last = [jnp.concatenate(packed[2 * k : 2 * k + 2], axis=1) for k in range(3)]
    gram = jnp.concatenate(
        [jnp.concatenate([first, cross.T], axis=1), jnp.concatenate([cross, last], axis=1)], axis=0
    )
    row = lax.broadcasted_iota(jnp.int32, (B, B), 0)
    column = lax.broadcasted_iota(jnp.int32, (B, B), 1)
    identity = jnp.where(row == column, 1.0, 0.0).astype(F32)
    damped = gram * (1.0 / 65536) + DAMPING * identity
    norm = jnp.max(jnp.sum(jnp.abs(damped), axis=1, keepdims=True), axis=0, keepdims=True)
    y = damped / norm
    ys = split(y)
    square = dot3(ys, ys)
    squares = split(square)
    z = 2.25 * identity - 2.4375 * y + 1.6875 * square + dot3(squares, split(0.0625 * square - 0.5625 * y))
    zs = split(z)
    root = 1.5 * z - 0.5 * dot3(split(dot3(zs, zs)), split(dot3(ys, zs)))
    root = (root / jnp.sqrt(norm)).astype(BF)
    out_ref[...] = jnp.dot(rows_ref[...], root, preferred_element_type=F32).astype(BF)


def local(activations, token_mask, gradient):
    core = lax.axis_index("core")
    mask = token_mask.astype(BF)[:, None]

    def columns(index):
        return lax.dynamic_slice(activations, (0, index * B), (activations.shape[0], B)) * mask

    other = lax.ppermute(columns(1 - core), "core", [(0, 1), (1, 0)])
    rows = gradient.shape[0]
    blocks = gradient.reshape(rows, SHARDS, B).transpose(1, 0, 2)
    blocks = lax.all_to_all(blocks, ("yh", "core"), 0, 0).reshape(SHARDS * rows, B)
    packed = call(gram_kernel, ((6, H, LANES), BF), columns(core), other).reshape(SHARDS, PACKED, LANES)
    for axes in (("x",), ("z", "yl")):
        packed = call(sum_kernel, (packed.shape, BF), lax.all_to_all(packed, axes, 0, 0))
    packed = lax.all_to_all(packed, "x", 0, 0).reshape(6, H, LANES)
    product = call(root_kernel, ((SHARDS * rows, B), BF), packed, blocks)
    product = lax.all_to_all(product.reshape(SHARDS, rows, B), ("yh", "core"), 0, 0)
    return product.transpose(1, 0, 2).reshape(rows, SHARDS * B)


def solution(mesh):
    names, sizes = zip(*AXES)
    cut = Mesh(mesh.devices.reshape(sizes), names)
    dp = names[:4]
    placed = (P(dp, "yh"), P(dp), P(names, None))
    return jax.shard_map(local, mesh=cut, in_specs=placed, out_specs=P(names, None), check_vma=False)
```

```python
import jax
import jax.numpy as jnp
from jax import lax
from jax.experimental import pallas as pl
from jax.experimental.pallas import tpu as pltpu
from jax.sharding import Mesh, PartitionSpec as P

B = 512
H = 256
LANES = 128
DAMPING = 0.05
BF = jnp.bfloat16
F32 = jnp.float32
AXES = (("z", 8), ("yl", 2), ("x", 4), ("core", 2), ("yh", 4))
REDUCE = ("z", "yl", "x")
SHARDS = 64
PACKED = 3 * 2 * H // SHARDS
ROWS = 32
TOKENS = 512
MASK_ROWS = 16
SLAB = TOKENS + 4 * ROWS + MASK_ROWS
VMEM = pl.BlockSpec(memory_space=pltpu.VMEM)
HBM = pl.BlockSpec(memory_space=pl.ANY)


def call(kernel, outs, operands, specs=None, scratch=(), flops=0):
    shapes = [jax.ShapeDtypeStruct(*out) for out in outs]
    moved = sum(o.size * o.dtype.itemsize for o in (*operands, *shapes))
    return pl.pallas_call(
        kernel,
        out_shape=shapes,
        in_specs=specs or [VMEM] * len(operands),
        out_specs=[VMEM] * len(outs),
        scratch_shapes=scratch,
        cost_estimate=pl.CostEstimate(flops=flops, bytes_accessed=moved, transcendentals=0),
        compiler_params=pltpu.CompilerParams(vmem_limit_bytes=40 * 1024 * 1024),
    )(*operands)


def at(index, size=B):
    return pl.ds(pl.multiple_of(index * size, size), size)


def slab_kernel(act_ref, mask_ref, grad_ref, out_ref, sems):
    other = 1 - lax.axis_index("core")
    copies = [pltpu.make_async_copy(act_ref.at[:, at(other)], out_ref.at[pl.ds(0, TOKENS)], sems.at[0])]
    for k in range(4):
        rows = pl.ds(TOKENS + ROWS * k, ROWS)
        copies.append(pltpu.make_async_copy(grad_ref.at[:, at(2 * k + other)], out_ref.at[rows], sems.at[k + 1]))
    for copy in copies:
        copy.start()
    mask = mask_ref[...].astype(F32).astype(BF)
    out_ref[pl.ds(TOKENS + 4 * ROWS, MASK_ROWS), :] = jnp.broadcast_to(mask, (MASK_ROWS, TOKENS))
    for copy in copies:
        copy.wait()


def masked(columns, mask):
    column = jnp.broadcast_to(mask.astype(F32), (LANES, TOKENS)).T.astype(BF)
    return columns * jnp.concatenate([column] * (B // LANES), axis=1)


def triangle(columns):
    dot = lambda a, b: lax.dot_general(a, b, (((0,), (0,)), ((), ())), preferred_element_type=F32)
    low, high = columns[:, :H], columns[:, H:]
    return dot(low, low), dot(high, low), dot(high, high)


def own_kernel(act_ref, mask_ref, out_ref, held, sem):
    copy = pltpu.make_async_copy(act_ref.at[:, at(lax.axis_index("core"))], held, sem)
    copy.start()
    mask = mask_ref[...].astype(F32)
    copy.wait()
    for slot, block in enumerate(triangle(masked(held[...], mask))):
        out_ref[slot] = block


def gram_kernel(slab_ref, own_ref, grad_ref, out_ref, send_ref, keep_ref):
    mask = slab_ref[pl.ds(TOKENS + 4 * ROWS, MASK_ROWS), :][:1]
    for slot, block in enumerate(triangle(masked(slab_ref[pl.ds(0, TOKENS), :], mask))):
        block += own_ref[slot]
        for half in range(2):
            out_ref[2 * slot + half] = block[:, half * LANES : (half + 1) * LANES].astype(BF)
    core = lax.axis_index("core")
    upper = lax.axis_index("yh") // 2
    for ref, part in ((send_ref, 1 - upper), (keep_ref, upper)):
        for k in range(2):
            ref[k, core] = grad_ref[:, at(2 * (2 * part + k) + core)]
            ref[k, 1 - core] = slab_ref[pl.ds(pl.multiple_of(TOKENS + ROWS * (2 * part + k), ROWS), ROWS), :]


def sum_kernel(parts_ref, kept_ref, come_ref, out_ref, send_ref, keep_ref):
    total = parts_ref[0].astype(F32)
    for part in range(1, SHARDS):
        total += parts_ref[part].astype(F32)
    rounded = total.astype(BF)
    for copy in range(SHARDS):
        out_ref[copy] = rounded
    upper, lower = lax.axis_index("yh") // 2, lax.axis_index("yh") % 2
    for ref, part in ((send_ref, 1 - lower), (keep_ref, lower)):
        ref[upper] = kept_ref[part]
        ref[1 - upper] = come_ref[part]


def split(array):
    high = array.astype(BF)
    return high, (array - high.astype(F32)).astype(BF)


def dot3(left, right):
    one = lambda a, b: jnp.dot(a, b, preferred_element_type=F32)
    return one(left[0], right[0]) + (one(left[0], right[1]) + one(left[1], right[0]))


def root_kernel(gram_ref, kept_ref, come_ref, out_ref):
    packed = [gram_ref[piece].astype(F32) for piece in range(6)]
    first, cross, last = [jnp.concatenate(packed[2 * k : 2 * k + 2], axis=1) for k in range(3)]
    gram = jnp.concatenate(
        [jnp.concatenate([first, cross.T], axis=1), jnp.concatenate([cross, last], axis=1)], axis=0
    )
    row = lax.broadcasted_iota(jnp.int32, (B, B), 0)
    column = lax.broadcasted_iota(jnp.int32, (B, B), 1)
    identity = jnp.where(row == column, 1.0, 0.0).astype(F32)
    damped = gram * (1.0 / 65536) + DAMPING * identity
    norm = jnp.max(jnp.sum(jnp.abs(damped), axis=1, keepdims=True), axis=0, keepdims=True)
    y = damped / norm
    ys = split(y)
    square = dot3(ys, ys)
    squares = split(square)
    z = 2.25 * identity - 2.4375 * y + 1.6875 * square + dot3(squares, split(0.0625 * square - 0.5625 * y))
    zs = split(z)
    root = 1.5 * z - 0.5 * dot3(split(dot3(zs, zs)), split(dot3(ys, zs)))
    root = (root / jnp.sqrt(norm)).astype(BF)
    lower = lax.axis_index("yh") % 2
    for ref, place in ((kept_ref, lower), (come_ref, 1 - lower)):
        product = jnp.dot(ref[...].reshape(4 * ROWS, B), root, preferred_element_type=F32).astype(BF)
        for upper in range(2):
            out_ref[upper, place] = product[2 * ROWS * upper : 2 * ROWS * (upper + 1)]


def local(activations, token_mask, gradient):
    mask = token_mask.reshape(1, TOKENS)
    dma = pltpu.SemaphoreType.DMA
    (slab,) = call(
        slab_kernel, [((SLAB, B), BF)], (activations, mask, gradient), [HBM, VMEM, HBM], [dma((5,))]
    )
    other = lax.ppermute(slab, "core", [(0, 1), (1, 0)])
    (own,) = call(
        own_kernel,
        [((3, H, H), F32)],
        (activations, mask),
        [HBM, VMEM],
        [pltpu.VMEM((TOKENS, B), BF), dma],
        flops=6 * TOKENS * H * H,
    )
    half = ((2, 2, ROWS, B), BF)
    packed, send, kept = call(
        gram_kernel, [((6, H, LANES), BF), half, half], (other, own, gradient), flops=6 * TOKENS * H * H
    )
    come = lax.ppermute(send, "yh", [(k, k ^ 2) for k in range(4)])
    parts = lax.all_to_all(packed.reshape(SHARDS, PACKED, LANES), REDUCE, 0, 0)
    copies, send, kept = call(sum_kernel, [(parts.shape, BF), half, half], (parts, kept, come))
    come = lax.ppermute(send, "yh", [(k, k ^ 1) for k in range(4)])
    packed = lax.all_to_all(copies, REDUCE, 0, 0).reshape(6, H, LANES)
    (product,) = call(
        root_kernel, [((2, 2, 2 * ROWS, B), BF)], (packed, kept, come), flops=2 * 16 * B * B * B
    )
    product = lax.all_to_all(product.reshape(8, ROWS, B), ("yh", "core"), 0, 0)
    return product.transpose(1, 0, 2).reshape(ROWS, 8 * B)


def solution(mesh):
    names, sizes = zip(*AXES)
    cut = Mesh(mesh.devices.reshape(sizes), names)
    dp = names[:4]
    placed = (P(dp, "yh"), P(dp), P(names, None))
    return jax.shard_map(local, mesh=cut, in_specs=placed, out_specs=P(names, None), check_vma=False)
```

```python
import jax
import jax.numpy as jnp
from jax import lax
from jax.experimental import pallas as pl
from jax.experimental.pallas import tpu as pltpu
from jax.sharding import Mesh, PartitionSpec as P

B = 512
H = 256
LANES = 128
DAMPING = 0.05
BF = jnp.bfloat16
F32 = jnp.float32
AXES = (("z", 8), ("yl", 2), ("x", 4), ("core", 2), ("yh", 4))
NAMES = tuple(name for name, _ in AXES)
PLANE = ("yl", "x")
SHARDS = 8
PACKED = 3 * 2 * H // SHARDS
ROWS = 32
TOKENS = 512
MASK_ROWS = 16
SLAB = TOKENS + 4 * ROWS + MASK_ROWS
VMEM_MIB = 16
VMEM = pl.BlockSpec(memory_space=pltpu.VMEM)
HBM = pl.BlockSpec(memory_space=pltpu.HBM)


def groups():
    at = lambda z, yl, x, core, yh: (((z * 2 + yl) * 4 + x) * 2 + core) * 4 + yh
    every = [(z, w, x) for z in range(8) for w in range(2) for x in range(4)]
    return [[at(z, w ^ (yh >> 1), x, core, yh) for yh in range(4) for core in range(2)] for z, w, x in every]


def pairs(flip):
    return [(group[2 * yh + core], group[2 * (yh ^ flip) + core]) for group in groups() for yh in range(4) for core in range(2)]


def call(kernel, outs, operands, specs=None, scratch=(), flops=0):
    shapes = [jax.ShapeDtypeStruct(*out) for out in outs]
    moved = sum(o.size * o.dtype.itemsize for o in (*operands, *shapes))
    return pl.pallas_call(
        kernel,
        out_shape=shapes,
        in_specs=specs or [VMEM] * len(operands),
        out_specs=[VMEM] * len(outs),
        scratch_shapes=scratch,
        cost_estimate=pl.CostEstimate(flops=flops, bytes_accessed=moved, transcendentals=0),
        compiler_params=pltpu.CompilerParams(vmem_limit_bytes=VMEM_MIB * 1024 * 1024),
    )(*operands)


def at(index, size=B):
    return pl.ds(pl.multiple_of(index * size, size), size)


def slab_kernel(act_ref, mask_ref, grad_ref, out_ref, mask_held, sems):
    other = 1 - lax.axis_index("core")
    copies = [pltpu.make_async_copy(act_ref.at[:, at(other)], out_ref.at[pl.ds(0, TOKENS)], sems.at[0])]
    for k in range(4):
        rows = pl.ds(TOKENS + ROWS * k, ROWS)
        copies.append(pltpu.make_async_copy(grad_ref.at[:, at(2 * k + other)], out_ref.at[rows], sems.at[k + 1]))
    copies.insert(0, pltpu.make_async_copy(mask_ref, mask_held, sems.at[5]))
    for copy in copies:
        copy.start()
    copies.pop(0).wait()
    mask = mask_held[...].astype(F32).astype(BF)
    out_ref[pl.ds(TOKENS + 4 * ROWS, MASK_ROWS), :] = jnp.broadcast_to(mask, (MASK_ROWS, TOKENS))
    for copy in copies:
        copy.wait()


def masked(columns, mask):
    column = jnp.broadcast_to(mask.astype(F32), (LANES, TOKENS)).T.astype(BF)
    return columns * jnp.concatenate([column] * (B // LANES), axis=1)


def triangle(columns):
    dot = lambda a, b: lax.dot_general(a, b, (((0,), (0,)), ((), ())), preferred_element_type=F32)
    low, high = columns[:, :H], columns[:, H:]
    return dot(low, low), dot(high, low), dot(high, high)


def own_kernel(act_ref, mask_ref, out_ref, held, mask_held, sems):
    columns = pltpu.make_async_copy(act_ref.at[:, at(lax.axis_index("core"))], held, sems.at[0])
    mask = pltpu.make_async_copy(mask_ref, mask_held, sems.at[1])
    columns.start()
    mask.start()
    columns.wait()
    mask.wait()
    for slot, block in enumerate(triangle(masked(held[...], mask_held[...]))):
        out_ref[slot] = block


def gram_kernel(slab_ref, own_ref, out_ref):
    mask = slab_ref[pl.ds(TOKENS + 4 * ROWS, MASK_ROWS), :][:1]
    for slot, block in enumerate(triangle(masked(slab_ref[pl.ds(0, TOKENS), :], mask))):
        block += own_ref[slot]
        for half in range(2):
            out_ref[2 * slot + half] = block[:, half * LANES : (half + 1) * LANES].astype(BF)


def first_kernel(slab_ref, grad_ref, send_ref, keep_ref, held, sem):
    copy = pltpu.make_async_copy(grad_ref, held, sem)
    copy.start()
    core, upper = lax.axis_index("core"), lax.axis_index("yh") // 2
    copy.wait()
    for ref, part in ((send_ref, 1 - upper), (keep_ref, upper)):
        for k in range(2):
            ref[k, core] = held[:, at(2 * (2 * part + k) + core)]
            ref[k, 1 - core] = slab_ref[pl.ds(pl.multiple_of(TOKENS + ROWS * (2 * part + k), ROWS), ROWS), :]


def spread(parts_ref, out_ref):
    total = parts_ref[0].astype(F32)
    for part in range(1, SHARDS):
        total += parts_ref[part].astype(F32)
    rounded = total.astype(BF)
    for copy in range(SHARDS):
        out_ref[copy] = rounded


def sum_kernel(parts_ref, kept_ref, come_ref, out_ref, send_ref, keep_ref):
    spread(parts_ref, out_ref)
    upper, lower = lax.axis_index("yh") // 2, lax.axis_index("yh") % 2
    for ref, part in ((send_ref, 1 - lower), (keep_ref, lower)):
        ref[upper] = kept_ref[part]
        ref[1 - upper] = come_ref[part]


def split(array):
    high = array.astype(BF)
    return high, (array - high.astype(F32)).astype(BF)


def dot3(left, right):
    one = lambda a, b: jnp.dot(a, b, preferred_element_type=F32)
    return one(left[0], right[0]) + (one(left[0], right[1]) + one(left[1], right[0]))


def root_kernel(gram_ref, out_ref):
    packed = [gram_ref[piece].astype(F32) for piece in range(6)]
    first, cross, last = [jnp.concatenate(packed[2 * k : 2 * k + 2], axis=1) for k in range(3)]
    gram = jnp.concatenate(
        [jnp.concatenate([first, cross.T], axis=1), jnp.concatenate([cross, last], axis=1)], axis=0
    )
    row = lax.broadcasted_iota(jnp.int32, (B, B), 0)
    column = lax.broadcasted_iota(jnp.int32, (B, B), 1)
    identity = jnp.where(row == column, 1.0, 0.0).astype(F32)
    damped = gram * (1.0 / 65536) + DAMPING * identity
    norm = jnp.max(jnp.sum(jnp.abs(damped), axis=1, keepdims=True), axis=0, keepdims=True)
    y = damped / norm
    ys = split(y)
    square = dot3(ys, ys)
    squares = split(square)
    z = 2.25 * identity - 2.4375 * y + 1.6875 * square + dot3(squares, split(0.0625 * square - 0.5625 * y))
    zs = split(z)
    root = 1.5 * z - 0.5 * dot3(split(dot3(zs, zs)), split(dot3(ys, zs)))
    out_ref[...] = (root / jnp.sqrt(norm)).astype(BF)


def apply_kernel(root_ref, kept_ref, come_ref, out_ref):
    turn = lax.axis_index("yh") // 2 + lax.axis_index("yh") % 2
    for ref, other in ((kept_ref, 0), (come_ref, 1)):
        product = jnp.dot(ref[...].reshape(4 * ROWS, B), root_ref[...], preferred_element_type=F32).astype(BF)
        for upper in range(2):
            out_ref[upper, (turn + upper + other) % 2] = product[2 * ROWS * upper : 2 * ROWS * (upper + 1)]


def local(activations, token_mask, gradient):
    mask = pltpu.with_memory_space_constraint(token_mask.reshape(1, TOKENS), pltpu.HBM)
    activations = pltpu.with_memory_space_constraint(activations, pltpu.HBM)
    gradient = pltpu.with_memory_space_constraint(gradient, pltpu.HBM)
    dma = pltpu.SemaphoreType.DMA
    (slab,) = call(
        slab_kernel, [((SLAB, B), BF)], (activations, mask, gradient), [HBM] * 3, [pltpu.VMEM((1, TOKENS), jnp.int32), dma((6,))]
    )
    other = lax.ppermute(slab, "core", [(0, 1), (1, 0)])
    (own,) = call(
        own_kernel,
        [((3, H, H), F32)],
        (activations, mask),
        [HBM, HBM],
        [pltpu.VMEM((TOKENS, B), BF), pltpu.VMEM((1, TOKENS), jnp.int32), dma((2,))],
        flops=6 * TOKENS * H * H,
    )
    half = ((2, 2, ROWS, B), BF)
    send, kept = call(
        first_kernel, [half, half], (other, gradient), [VMEM, HBM], [pltpu.VMEM((ROWS, 8 * B), BF), dma]
    )
    come = lax.ppermute(send, NAMES, pairs(3))
    (packed,) = call(gram_kernel, [((6, H, LANES), BF)], (other, own), flops=6 * TOKENS * H * H)
    parts = lax.all_to_all(packed.reshape(SHARDS, PACKED, LANES), PLANE, 0, 0)
    (copies,) = call(spread, [(parts.shape, BF)], (parts,))
    parts = lax.all_to_all(copies, "z", 0, 0)
    copies, send, kept = call(sum_kernel, [(parts.shape, BF), half, half], (parts, kept, come))
    come = lax.ppermute(send, NAMES, pairs(1))
    packed = lax.all_to_all(copies, PLANE, 0, 0).reshape(6, H, LANES)
    (root,) = call(root_kernel, [((B, B), BF)], (packed,), flops=2 * 15 * B * B * B)
    (product,) = call(apply_kernel, [((2, 2, 2 * ROWS, B), BF)], (root, kept, come), flops=2 * 8 * ROWS * B * B)
    product = lax.all_to_all(product.reshape(8, ROWS, B), NAMES, 0, 0, axis_index_groups=groups())
    return product.transpose(1, 0, 2).reshape(ROWS, 8 * B)


def solution(mesh):
    names, sizes = zip(*AXES)
    cut = Mesh(mesh.devices.reshape(sizes), names)
    dp = names[:4]
    placed = (P(dp, "yh"), P(dp), P(names, None))
    return jax.shard_map(local, mesh=cut, in_specs=placed, out_specs=P(names, None), check_vma=False)
```

```python
import jax
import jax.numpy as jnp
from jax import lax
from jax.experimental import pallas as pl
from jax.experimental.pallas import tpu as pltpu
from jax.sharding import Mesh, PartitionSpec as P

B = 512
H = 256
LANES = 128
DAMPING = 0.05
BF = jnp.bfloat16
F32 = jnp.float32
AXES = (("z", 8), ("yl", 2), ("x", 4), ("core", 2), ("yh", 4))
NAMES = tuple(name for name, _ in AXES)
PLANE = ("yl", "x")
SHARDS = 8
TRIANGLE = [(row, column) for column in range(4) for row in range(column, 4)]
PACKED = len(TRIANGLE) * LANES // SHARDS
ROWS = 32
TOKENS = 512
MASK_ROWS = 16
SLAB = TOKENS + 4 * ROWS + MASK_ROWS
VMEM_MIB = 16
VMEM = pl.BlockSpec(memory_space=pltpu.VMEM)
HBM = pl.BlockSpec(memory_space=pltpu.HBM)


def groups():
    at = lambda z, yl, x, core, yh: (((z * 2 + yl) * 4 + x) * 2 + core) * 4 + yh
    every = [(z, w, x) for z in range(8) for w in range(2) for x in range(4)]
    return [[at(z, w ^ (yh >> 1), x, core, yh) for yh in range(4) for core in range(2)] for z, w, x in every]


def pairs(flip):
    return [(group[2 * yh + core], group[2 * (yh ^ flip) + core]) for group in groups() for yh in range(4) for core in range(2)]


def call(kernel, outs, operands, specs=None, scratch=(), flops=0):
    shapes = [jax.ShapeDtypeStruct(*out) for out in outs]
    moved = sum(o.size * o.dtype.itemsize for o in (*operands, *shapes))
    return pl.pallas_call(
        kernel,
        out_shape=shapes,
        in_specs=specs or [VMEM] * len(operands),
        out_specs=[VMEM] * len(outs),
        scratch_shapes=scratch,
        cost_estimate=pl.CostEstimate(flops=flops, bytes_accessed=moved, transcendentals=0),
        compiler_params=pltpu.CompilerParams(vmem_limit_bytes=VMEM_MIB * 1024 * 1024),
    )(*operands)


def at(index, size=B):
    return pl.ds(pl.multiple_of(index * size, size), size)


def slab_kernel(act_ref, mask_ref, grad_ref, out_ref, mine_ref, mask_held, sems):
    other = 1 - lax.axis_index("core")
    copies = [pltpu.make_async_copy(act_ref.at[:, at(other)], out_ref.at[pl.ds(0, TOKENS)], sems.at[0])]
    for k in range(4):
        rows = pl.ds(TOKENS + ROWS * k, ROWS)
        copies.append(pltpu.make_async_copy(grad_ref.at[:, at(2 * k + other)], out_ref.at[rows], sems.at[k + 1]))
        rows = pl.ds(ROWS * k, ROWS)
        copies.append(pltpu.make_async_copy(grad_ref.at[:, at(2 * k + 1 - other)], mine_ref.at[rows], sems.at[k + 6]))
    copies.insert(0, pltpu.make_async_copy(mask_ref, mask_held, sems.at[5]))
    for copy in copies:
        copy.start()
    copies.pop(0).wait()
    mask = mask_held[...].astype(F32).astype(BF)
    out_ref[pl.ds(TOKENS + 4 * ROWS, MASK_ROWS), :] = jnp.broadcast_to(mask, (MASK_ROWS, TOKENS))
    for copy in copies:
        copy.wait()


def masked(columns, mask):
    column = jnp.broadcast_to(mask.astype(F32), (LANES, TOKENS)).T.astype(BF)
    return columns * jnp.concatenate([column] * (B // LANES), axis=1)


def triangle(columns):
    dot = lambda a, b: lax.dot_general(a, b, (((0,), (0,)), ((), ())), preferred_element_type=F32)
    low, high = columns[:, :H], columns[:, H:]
    return dot(low, low), dot(high, low), dot(high, high)


def own_kernel(act_ref, mask_ref, out_ref, held, mask_held, sems):
    columns = pltpu.make_async_copy(act_ref.at[:, at(lax.axis_index("core"))], held, sems.at[0])
    mask = pltpu.make_async_copy(mask_ref, mask_held, sems.at[1])
    columns.start()
    mask.start()
    columns.wait()
    mask.wait()
    for slot, block in enumerate(triangle(masked(held[...], mask_held[...]))):
        out_ref[slot] = block


def gram_kernel(slab_ref, own_ref, out_ref):
    mask = slab_ref[pl.ds(TOKENS + 4 * ROWS, MASK_ROWS), :][:1]
    blocks = triangle(masked(slab_ref[pl.ds(0, TOKENS), :], mask))
    blocks = [block + own_ref[slot] for slot, block in enumerate(blocks)]
    for piece, (row, column) in enumerate(TRIANGLE):
        block = blocks[row // 2 + column // 2]
        row, column = LANES * (row % 2), LANES * (column % 2)
        out_ref[piece] = block[row : row + LANES, column : column + LANES].astype(BF)


def first_kernel(slab_ref, mine_ref, send_ref, keep_ref):
    core, upper = lax.axis_index("core"), lax.axis_index("yh") // 2
    for ref, part in ((send_ref, 1 - upper), (keep_ref, upper)):
        for k in range(2):
            ref[k, core] = mine_ref[at(2 * part + k, ROWS), :]
            ref[k, 1 - core] = slab_ref[pl.ds(pl.multiple_of(TOKENS + ROWS * (2 * part + k), ROWS), ROWS), :]


def spread(parts_ref, out_ref):
    total = parts_ref[0].astype(F32)
    for part in range(1, SHARDS):
        total += parts_ref[part].astype(F32)
    rounded = total.astype(BF)
    for copy in range(SHARDS):
        out_ref[copy] = rounded


def sum_kernel(parts_ref, kept_ref, come_ref, out_ref, send_ref, keep_ref):
    spread(parts_ref, out_ref)
    upper, lower = lax.axis_index("yh") // 2, lax.axis_index("yh") % 2
    for ref, part in ((send_ref, 1 - lower), (keep_ref, lower)):
        ref[upper] = kept_ref[part]
        ref[1 - upper] = come_ref[part]


def root_kernel(gram_ref, out_ref):
    pieces = {place: gram_ref[piece].astype(F32) for piece, place in enumerate(TRIANGLE)}
    entry = lambda row, column: pieces[row, column] if row >= column else pieces[column, row].T
    gram = jnp.concatenate(
        [jnp.concatenate([entry(row, column) for column in range(4)], axis=1) for row in range(4)], axis=0
    )
    row = lax.broadcasted_iota(jnp.int32, (B, B), 0)
    column = lax.broadcasted_iota(jnp.int32, (B, B), 1)
    identity = jnp.where(row == column, 1.0, 0.0).astype(F32)
    damped = gram * (1.0 / 65536) + DAMPING * identity
    norm = jnp.max(jnp.sum(jnp.abs(damped), axis=1, keepdims=True), axis=0, keepdims=True)
    dot = lambda left, right: jnp.dot(left, right, preferred_element_type=F32)
    y = damped * (1.0 / norm)
    near = y.astype(BF)
    square = dot(near, near)
    z = 2.25 * identity - 2.4375 * y + 1.6875 * square + dot(square.astype(BF), (0.0625 * square - 0.5625 * y).astype(BF))
    close = z.astype(BF)
    root = 1.5 * z - 0.5 * dot(dot(close, close).astype(BF), dot(near, close).astype(BF))
    out_ref[...] = (root * (1.0 / jnp.sqrt(norm))).astype(BF)


def apply_kernel(root_ref, kept_ref, come_ref, out_ref):
    turn = lax.axis_index("yh") // 2 + lax.axis_index("yh") % 2
    for ref, other in ((kept_ref, 0), (come_ref, 1)):
        product = jnp.dot(ref[...].reshape(4 * ROWS, B), root_ref[...], preferred_element_type=F32).astype(BF)
        for upper in range(2):
            out_ref[upper, (turn + upper + other) % 2] = product[2 * ROWS * upper : 2 * ROWS * (upper + 1)]


def local(activations, token_mask, gradient):
    mask = pltpu.with_memory_space_constraint(token_mask.reshape(1, TOKENS), pltpu.HBM)
    activations = pltpu.with_memory_space_constraint(activations, pltpu.HBM)
    gradient = pltpu.with_memory_space_constraint(gradient, pltpu.HBM)
    dma = pltpu.SemaphoreType.DMA
    slab, mine = call(
        slab_kernel, [((SLAB, B), BF), ((4 * ROWS, B), BF)], (activations, mask, gradient), [HBM] * 3, [pltpu.VMEM((1, TOKENS), jnp.int32), dma((10,))]
    )
    other = lax.ppermute(slab, "core", [(0, 1), (1, 0)])
    (own,) = call(
        own_kernel,
        [((3, H, H), F32)],
        (activations, mask),
        [HBM, HBM],
        [pltpu.VMEM((TOKENS, B), BF), pltpu.VMEM((1, TOKENS), jnp.int32), dma((2,))],
        flops=6 * TOKENS * H * H,
    )
    half = ((2, 2, ROWS, B), BF)
    send, kept = call(first_kernel, [half, half], (other, mine))
    come = lax.ppermute(send, NAMES, pairs(3))
    (packed,) = call(gram_kernel, [((len(TRIANGLE), LANES, LANES), BF)], (other, own), flops=6 * TOKENS * H * H)
    parts = lax.all_to_all(packed.reshape(SHARDS, PACKED, LANES), PLANE, 0, 0)
    (copies,) = call(spread, [(parts.shape, BF)], (parts,))
    parts = lax.all_to_all(copies, "z", 0, 0)
    copies, send, kept = call(sum_kernel, [(parts.shape, BF), half, half], (parts, kept, come))
    come = lax.ppermute(send, NAMES, pairs(1))
    packed = lax.all_to_all(copies, PLANE, 0, 0).reshape(len(TRIANGLE), LANES, LANES)
    (root,) = call(root_kernel, [((B, B), BF)], (packed,), flops=2 * 5 * B * B * B)
    (product,) = call(apply_kernel, [((2, 2, 2 * ROWS, B), BF)], (root, kept, come), flops=2 * 8 * ROWS * B * B)
    product = lax.all_to_all(product.reshape(8, ROWS, B), NAMES, 0, 0, axis_index_groups=groups())
    return product.transpose(1, 0, 2).reshape(ROWS, 8 * B)


def solution(mesh):
    names, sizes = zip(*AXES)
    cut = Mesh(mesh.devices.reshape(sizes), names)
    dp = names[:4]
    placed = (P(dp, "yh"), P(dp), P(names, None))
    return jax.shard_map(local, mesh=cut, in_specs=placed, out_specs=P(names, None), check_vma=False)
```

```python
import itertools

import jax
import jax.numpy as jnp
from jax import lax
from jax.experimental import pallas as pl
from jax.experimental.pallas import tpu as pltpu
from jax.sharding import Mesh, PartitionSpec as P

B = 512
H = 256
LANES = 128
DAMPING = 0.05
BF = jnp.bfloat16
F32 = jnp.float32
AXES = (("z", 8), ("yl", 2), ("x", 4), ("core", 2), ("yh", 4))
NAMES = tuple(name for name, _ in AXES)
SHARDS = 8
TRIANGLE = [(row, column) for column in range(4) for row in range(column, 4)]
PACKED = len(TRIANGLE) * LANES // SHARDS
ROWS = 32
TOKENS = 512
MASK_ROWS = 16
ZFIRST = 7
PFIRST = (1, 2)
ORDER = (2, 3, 0, 1)
SLAB = TOKENS + 4 * ROWS + MASK_ROWS
VMEM_MIB = 16
VMEM = pl.BlockSpec(memory_space=pltpu.VMEM)
HBM = pl.BlockSpec(memory_space=pltpu.HBM)


def place(z, yl, x, core, yh):
    return (((z * 2 + yl) * 4 + x) * 2 + core) * 4 + yh


def groups():
    every = [(z, w, x) for z in range(8) for w in range(2) for x in range(4)]
    return [[place(z, w ^ (yh >> 1), x, core, yh) for yh in ORDER for core in range(2)] for z, w, x in every]


def layers():
    order = (ZFIRST, *[z for z in range(8) if z != ZFIRST])
    rests = itertools.product(range(2), range(4), range(2), range(4))
    return [[place(z, *rest) for z in order] for rest in rests]


def planes():
    spots = [(yl ^ PFIRST[0], x ^ PFIRST[1]) for yl in range(2) for x in range(4)]
    return [[place(z, yl, x, core, yh) for yl, x in spots] for z in range(8) for core in range(2) for yh in range(4)]


def pairs(flip):
    spot = {yh: k for k, yh in enumerate(ORDER)}
    ends = [(2 * spot[yh] + core, 2 * spot[yh ^ flip] + core) for yh in range(4) for core in range(2)]
    return [(group[source], group[target]) for group in groups() for source, target in ends]


def call(kernel, outs, operands, specs=None, scratch=(), flops=0):
    shapes = [jax.ShapeDtypeStruct(*out) for out in outs]
    moved = sum(o.size * o.dtype.itemsize for o in (*operands, *shapes))
    return pl.pallas_call(
        kernel,
        out_shape=shapes,
        in_specs=specs or [VMEM] * len(operands),
        out_specs=[VMEM] * len(outs),
        scratch_shapes=scratch,
        cost_estimate=pl.CostEstimate(flops=flops, bytes_accessed=moved, transcendentals=0),
        compiler_params=pltpu.CompilerParams(vmem_limit_bytes=VMEM_MIB * 1024 * 1024),
    )(*operands)


def at(index, size=B):
    return pl.ds(pl.multiple_of(index * size, size), size)


def slab_kernel(act_ref, mask_ref, grad_ref, out_ref, mine_ref, mask_held, sems):
    other = 1 - lax.axis_index("core")
    copies = [pltpu.make_async_copy(act_ref.at[:, at(other)], out_ref.at[pl.ds(0, TOKENS)], sems.at[0])]
    for k in range(4):
        rows = pl.ds(TOKENS + ROWS * k, ROWS)
        copies.append(pltpu.make_async_copy(grad_ref.at[:, at(2 * k + other)], out_ref.at[rows], sems.at[k + 1]))
        rows = pl.ds(ROWS * k, ROWS)
        copies.append(pltpu.make_async_copy(grad_ref.at[:, at(2 * k + 1 - other)], mine_ref.at[rows], sems.at[k + 6]))
    copies.insert(0, pltpu.make_async_copy(mask_ref, mask_held, sems.at[5]))
    for copy in copies:
        copy.start()
    copies.pop(0).wait()
    mask = mask_held[...].astype(F32).astype(BF)
    out_ref[pl.ds(TOKENS + 4 * ROWS, MASK_ROWS), :] = jnp.broadcast_to(mask, (MASK_ROWS, TOKENS))
    for copy in copies:
        copy.wait()


def masked(columns, mask):
    column = jnp.broadcast_to(mask.astype(F32), (LANES, TOKENS)).T.astype(BF)
    return columns * jnp.concatenate([column] * (B // LANES), axis=1)


def triangle(columns):
    dot = lambda a, b: lax.dot_general(a, b, (((0,), (0,)), ((), ())), preferred_element_type=F32)
    low, high = columns[:, :H], columns[:, H:]
    return dot(low, low), dot(high, low), dot(high, high)


def own_kernel(act_ref, mask_ref, out_ref, held, mask_held, sems):
    columns = pltpu.make_async_copy(act_ref.at[:, at(lax.axis_index("core"))], held, sems.at[0])
    mask = pltpu.make_async_copy(mask_ref, mask_held, sems.at[1])
    columns.start()
    mask.start()
    columns.wait()
    mask.wait()
    for slot, block in enumerate(triangle(masked(held[...], mask_held[...]))):
        out_ref[slot] = block


def gram_kernel(slab_ref, own_ref, out_ref):
    mask = slab_ref[pl.ds(TOKENS + 4 * ROWS, MASK_ROWS), :][:1]
    blocks = triangle(masked(slab_ref[pl.ds(0, TOKENS), :], mask))
    blocks = [block + own_ref[slot] for slot, block in enumerate(blocks)]
    for piece, (row, column) in enumerate(TRIANGLE):
        block = blocks[row // 2 + column // 2]
        row, column = LANES * (row % 2), LANES * (column % 2)
        out_ref[piece] = block[row : row + LANES, column : column + LANES].astype(BF)


def spread(parts_ref, out_ref):
    total = parts_ref[0].astype(F32)
    for part in range(1, SHARDS):
        total += parts_ref[part].astype(F32)
    rounded = total.astype(BF)
    for copy in range(SHARDS):
        out_ref[copy] = rounded


def first_sum(parts_ref, slab_ref, mine_ref, out_ref, send_ref, keep_ref):
    spread(parts_ref, out_ref)
    core, upper = lax.axis_index("core"), lax.axis_index("yh") // 2
    for ref, part in ((send_ref, 1 - upper), (keep_ref, upper)):
        for k in range(2):
            ref[k, core] = mine_ref[at(2 * part + k, ROWS), :]
            ref[k, 1 - core] = slab_ref[pl.ds(pl.multiple_of(TOKENS + ROWS * (2 * part + k), ROWS), ROWS), :]


def sum_kernel(parts_ref, kept_ref, come_ref, out_ref, send_ref, keep_ref):
    spread(parts_ref, out_ref)
    upper, lower = lax.axis_index("yh") // 2, lax.axis_index("yh") % 2
    for ref, part in ((send_ref, 1 - lower), (keep_ref, lower)):
        ref[upper] = kept_ref[part]
        ref[1 - upper] = come_ref[part]


def root_kernel(gram_ref, out_ref):
    pieces = {place: gram_ref[piece].astype(F32) for piece, place in enumerate(TRIANGLE)}
    entry = lambda row, column: pieces[row, column] if row >= column else pieces[column, row].T
    gram = jnp.concatenate(
        [jnp.concatenate([entry(row, column) for column in range(4)], axis=1) for row in range(4)], axis=0
    )
    row = lax.broadcasted_iota(jnp.int32, (B, B), 0)
    column = lax.broadcasted_iota(jnp.int32, (B, B), 1)
    identity = jnp.where(row == column, 1.0, 0.0).astype(F32)
    damped = gram * (1.0 / 65536) + DAMPING * identity
    norm = jnp.max(jnp.sum(jnp.abs(damped), axis=1, keepdims=True), axis=0, keepdims=True)
    dot = lambda left, right: jnp.dot(left, right, preferred_element_type=F32)
    y = damped * (1.0 / norm)
    near = y.astype(BF)
    square = dot(near, near)
    z = 2.25 * identity - 2.4375 * y + 1.6875 * square + dot(square.astype(BF), (0.0625 * square - 0.5625 * y).astype(BF))
    close = z.astype(BF)
    both = dot(jnp.concatenate([close, near], axis=0), close).astype(BF)
    root = 1.5 * z - 0.5 * dot(both[:B], both[B:])
    out_ref[...] = (root * (1.0 / jnp.sqrt(norm))).astype(BF)


def apply_kernel(root_ref, kept_ref, come_ref, out_ref):
    turn = lax.axis_index("yh") // 2 + lax.axis_index("yh") % 2
    for ref, other in ((kept_ref, 0), (come_ref, 1)):
        product = jnp.dot(ref[...].reshape(4 * ROWS, B), root_ref[...], preferred_element_type=F32).astype(BF)
        for upper in range(2):
            out_ref[1 - upper, (turn + upper + other) % 2] = product[2 * ROWS * upper : 2 * ROWS * (upper + 1)]


def local(activations, token_mask, gradient):
    mask = pltpu.with_memory_space_constraint(token_mask.reshape(1, TOKENS), pltpu.HBM)
    activations = pltpu.with_memory_space_constraint(activations, pltpu.HBM)
    gradient = pltpu.with_memory_space_constraint(gradient, pltpu.HBM)
    dma = pltpu.SemaphoreType.DMA
    slab, mine = call(
        slab_kernel,
        [((SLAB, B), BF), ((4 * ROWS, B), BF)],
        (activations, mask, gradient),
        [HBM] * 3,
        [pltpu.VMEM((1, TOKENS), jnp.int32), dma((10,))],
    )
    other = lax.ppermute(slab, "core", [(0, 1), (1, 0)])
    (own,) = call(
        own_kernel,
        [((3, H, H), F32)],
        (activations, mask),
        [HBM, HBM],
        [pltpu.VMEM((TOKENS, B), BF), pltpu.VMEM((1, TOKENS), jnp.int32), dma((2,))],
        flops=6 * TOKENS * H * H,
    )
    half = ((2, 2, ROWS, B), BF)
    (packed,) = call(gram_kernel, [((len(TRIANGLE), LANES, LANES), BF)], (other, own), flops=6 * TOKENS * H * H)
    parts = lax.all_to_all(packed.reshape(SHARDS, PACKED, LANES), NAMES, 0, 0, axis_index_groups=planes())
    copies, send, kept = call(first_sum, [(parts.shape, BF), half, half], (parts, other, mine))
    come = lax.ppermute(send, NAMES, pairs(3))
    parts = lax.all_to_all(copies, NAMES, 0, 0, axis_index_groups=layers())
    copies, send, kept = call(sum_kernel, [(parts.shape, BF), half, half], (parts, kept, come))
    come = lax.ppermute(send, NAMES, pairs(1))
    packed = lax.all_to_all(copies, NAMES, 0, 0, axis_index_groups=planes()).reshape(len(TRIANGLE), LANES, LANES)
    (root,) = call(root_kernel, [((B, B), BF)], (packed,), flops=2 * 5 * B * B * B)
    (product,) = call(apply_kernel, [((2, 2, 2 * ROWS, B), BF)], (root, kept, come), flops=2 * 8 * ROWS * B * B)
    product = lax.all_to_all(product.reshape(8, ROWS, B), NAMES, 0, 0, axis_index_groups=groups())
    product = jnp.concatenate([product[4:], product[:4]], axis=0)
    return product.transpose(1, 0, 2).reshape(ROWS, 8 * B)


def solution(mesh):
    names, sizes = zip(*AXES)
    cut = Mesh(mesh.devices.reshape(sizes), names)
    dp = names[:4]
    placed = (P(dp, "yh"), P(dp), P(names, None))
    return jax.shard_map(local, mesh=cut, in_specs=placed, out_specs=P(names, None), check_vma=False)
```

```python
import itertools

import jax
import jax.numpy as jnp
from jax import lax
from jax.experimental import pallas as pl
from jax.experimental.pallas import tpu as pltpu
from jax.sharding import Mesh, PartitionSpec as P

B = 512
H = 256
LANES = 128
DAMPING = 0.05
BF = jnp.bfloat16
F32 = jnp.float32
AXES = (("z", 8), ("yl", 2), ("x", 4), ("core", 2), ("yh", 4))
NAMES = tuple(name for name, _ in AXES)
SHARDS = 8
TRIANGLE = [(row, column) for column in range(4) for row in range(column, 4)]
PACKED = len(TRIANGLE) * LANES // SHARDS
ROWS = 32
TOKENS = 512
MASK_ROWS = 16
ZFIRST = 6
SCATTER = 6
GATHER = 1
RETURN = 2
SLAB = TOKENS + 4 * ROWS + MASK_ROWS
VMEM_MIB = 16
VMEM = pl.BlockSpec(memory_space=pltpu.VMEM)
HBM = pl.BlockSpec(memory_space=pltpu.HBM)


def place(z, yl, x, core, yh):
    return (((z * 2 + yl) * 4 + x) * 2 + core) * 4 + yh


def groups():
    orders = [k ^ RETURN for k in range(4)]
    every = [(z, w, x) for z in range(8) for w in range(2) for x in range(4)]
    return [[place(z, w ^ (yh >> 1), x, core, yh) for yh in orders for core in range(2)] for z, w, x in every]


def layers():
    order = (ZFIRST, *[z for z in range(8) if z != ZFIRST])
    rests = itertools.product(range(2), range(4), range(2), range(4))
    return [[place(z, *rest) for z in order] for rest in rests]


def planes(first):
    spots = [divmod(k ^ first, 4) for k in range(SHARDS)]
    return [[place(z, yl, x, core, yh) for yl, x in spots] for z in range(8) for core in range(2) for yh in range(4)]


def pairs(flip):
    ends = [(2 * yh + core, 2 * (yh ^ flip) + core) for yh in range(4) for core in range(2)]
    return [(group[source], group[target]) for group in groups() for source, target in ends]


def call(kernel, outs, operands, specs=None, scratch=(), flops=0):
    shapes = [jax.ShapeDtypeStruct(*out) for out in outs]
    moved = sum(o.size * o.dtype.itemsize for o in (*operands, *shapes))
    return pl.pallas_call(
        kernel,
        out_shape=shapes,
        in_specs=specs or [VMEM] * len(operands),
        out_specs=[VMEM] * len(outs),
        scratch_shapes=scratch,
        cost_estimate=pl.CostEstimate(flops=flops, bytes_accessed=moved, transcendentals=0),
        compiler_params=pltpu.CompilerParams(vmem_limit_bytes=VMEM_MIB * 1024 * 1024),
    )(*operands)


def at(index, size=B):
    return pl.ds(pl.multiple_of(index * size, size), size)


def slab_kernel(act_ref, mask_ref, grad_ref, out_ref, mine_ref, mask_held, sems):
    other = 1 - lax.axis_index("core")
    copies = [pltpu.make_async_copy(act_ref.at[:, at(other)], out_ref.at[pl.ds(0, TOKENS)], sems.at[0])]
    for k in range(4):
        rows = pl.ds(TOKENS + ROWS * k, ROWS)
        copies.append(pltpu.make_async_copy(grad_ref.at[:, at(2 * k + other)], out_ref.at[rows], sems.at[k + 1]))
        rows = pl.ds(ROWS * k, ROWS)
        copies.append(pltpu.make_async_copy(grad_ref.at[:, at(2 * k + 1 - other)], mine_ref.at[rows], sems.at[k + 6]))
    copies.insert(0, pltpu.make_async_copy(mask_ref, mask_held, sems.at[5]))
    for copy in copies:
        copy.start()
    copies.pop(0).wait()
    mask = mask_held[...].astype(F32).astype(BF)
    out_ref[pl.ds(TOKENS + 4 * ROWS, MASK_ROWS), :] = jnp.broadcast_to(mask, (MASK_ROWS, TOKENS))
    for copy in copies:
        copy.wait()


def masked(columns, mask):
    column = jnp.broadcast_to(mask.astype(F32), (LANES, TOKENS)).T.astype(BF)
    return columns * jnp.concatenate([column] * (B // LANES), axis=1)


def triangle(columns):
    dot = lambda a, b: lax.dot_general(a, b, (((0,), (0,)), ((), ())), preferred_element_type=F32)
    low, high = columns[:, :H], columns[:, H:]
    return dot(low, low), dot(high, low), dot(high, high)


def own_kernel(act_ref, mask_ref, out_ref, held, mask_held, sems):
    columns = pltpu.make_async_copy(act_ref.at[:, at(lax.axis_index("core"))], held, sems.at[0])
    mask = pltpu.make_async_copy(mask_ref, mask_held, sems.at[1])
    columns.start()
    mask.start()
    columns.wait()
    mask.wait()
    for slot, block in enumerate(triangle(masked(held[...], mask_held[...]))):
        out_ref[slot] = block


def gram_kernel(slab_ref, own_ref, out_ref):
    mask = slab_ref[pl.ds(TOKENS + 4 * ROWS, MASK_ROWS), :][:1]
    blocks = triangle(masked(slab_ref[pl.ds(0, TOKENS), :], mask))
    blocks = [block + own_ref[slot] for slot, block in enumerate(blocks)]
    for piece, (row, column) in enumerate(TRIANGLE):
        block = blocks[row // 2 + column // 2]
        row, column = LANES * (row % 2), LANES * (column % 2)
        out_ref[piece] = block[row : row + LANES, column : column + LANES].astype(BF)


def spread(parts_ref, out_ref):
    total = parts_ref[0].astype(F32)
    for part in range(1, SHARDS):
        total += parts_ref[part].astype(F32)
    rounded = total.astype(BF)
    for copy in range(SHARDS):
        out_ref[copy] = rounded


def first_sum(parts_ref, slab_ref, mine_ref, out_ref, send_ref, keep_ref):
    spread(parts_ref, out_ref)
    core, upper = lax.axis_index("core"), lax.axis_index("yh") // 2
    for ref, part in ((send_ref, 1 - upper), (keep_ref, upper)):
        for k in range(2):
            ref[k, core] = mine_ref[at(2 * part + k, ROWS), :]
            ref[k, 1 - core] = slab_ref[pl.ds(pl.multiple_of(TOKENS + ROWS * (2 * part + k), ROWS), ROWS), :]


def sum_kernel(parts_ref, kept_ref, come_ref, out_ref, send_ref, keep_ref):
    spread(parts_ref, out_ref)
    upper, lower = lax.axis_index("yh") // 2, lax.axis_index("yh") % 2
    for ref, part in ((send_ref, 1 - lower), (keep_ref, lower)):
        ref[upper] = kept_ref[part]
        ref[1 - upper] = come_ref[part]


def root_kernel(gram_ref, out_ref):
    shards = [gram_ref[spot ^ SCATTER ^ GATHER] for spot in range(SHARDS)]
    packed = jnp.concatenate(shards, axis=0).astype(F32)
    pieces = {spot: packed[LANES * piece : LANES * (piece + 1)] for piece, spot in enumerate(TRIANGLE)}
    entry = lambda row, column: pieces[row, column] if row >= column else pieces[column, row].T
    gram = jnp.concatenate(
        [jnp.concatenate([entry(row, column) for column in range(4)], axis=1) for row in range(4)], axis=0
    )
    row = lax.broadcasted_iota(jnp.int32, (B, B), 0)
    column = lax.broadcasted_iota(jnp.int32, (B, B), 1)
    identity = jnp.where(row == column, 1.0, 0.0).astype(F32)
    damped = gram * (1.0 / 65536) + DAMPING * identity
    norm = jnp.max(jnp.sum(jnp.abs(damped), axis=1, keepdims=True), axis=0, keepdims=True)
    dot = lambda left, right: jnp.dot(left, right, preferred_element_type=F32)
    y = damped * (1.0 / norm)
    near = y.astype(BF)
    square = dot(near, near)
    z = 2.25 * identity - 2.4375 * y + 1.6875 * square + dot(square.astype(BF), (0.0625 * square - 0.5625 * y).astype(BF))
    close = z.astype(BF)
    both = dot(jnp.concatenate([close, near], axis=0), close).astype(BF)
    root = 1.5 * z - 0.5 * dot(both[:B], both[B:])
    out_ref[...] = (root * (1.0 / jnp.sqrt(norm))).astype(BF)


def apply_kernel(root_ref, kept_ref, come_ref, out_ref):
    turn = lax.axis_index("yh") // 2 + lax.axis_index("yh") % 2
    for ref, other in ((kept_ref, 0), (come_ref, 1)):
        product = jnp.dot(ref[...].reshape(4 * ROWS, B), root_ref[...], preferred_element_type=F32).astype(BF)
        for upper in range(2):
            out_ref[upper ^ (RETURN >> 1), (turn + upper + other + RETURN) % 2] = product[2 * ROWS * upper : 2 * ROWS * (upper + 1)]


def local(activations, token_mask, gradient):
    mask = pltpu.with_memory_space_constraint(token_mask.reshape(1, TOKENS), pltpu.HBM)
    activations = pltpu.with_memory_space_constraint(activations, pltpu.HBM)
    gradient = pltpu.with_memory_space_constraint(gradient, pltpu.HBM)
    dma = pltpu.SemaphoreType.DMA
    slab, mine = call(
        slab_kernel,
        [((SLAB, B), BF), ((4 * ROWS, B), BF)],
        (activations, mask, gradient),
        [HBM] * 3,
        [pltpu.VMEM((1, TOKENS), jnp.int32), dma((10,))],
    )
    other = lax.ppermute(slab, "core", [(0, 1), (1, 0)])
    (own,) = call(
        own_kernel,
        [((3, H, H), F32)],
        (activations, mask),
        [HBM, HBM],
        [pltpu.VMEM((TOKENS, B), BF), pltpu.VMEM((1, TOKENS), jnp.int32), dma((2,))],
        flops=6 * TOKENS * H * H,
    )
    half = ((2, 2, ROWS, B), BF)
    (packed,) = call(gram_kernel, [((len(TRIANGLE), LANES, LANES), BF)], (other, own), flops=6 * TOKENS * H * H)
    parts = lax.all_to_all(packed.reshape(SHARDS, PACKED, LANES), NAMES, 0, 0, axis_index_groups=planes(SCATTER))
    copies, send, kept = call(first_sum, [(parts.shape, BF), half, half], (parts, other, mine))
    come = lax.ppermute(send, NAMES, pairs(3))
    parts = lax.all_to_all(copies, NAMES, 0, 0, axis_index_groups=layers())
    copies, send, kept = call(sum_kernel, [(parts.shape, BF), half, half], (parts, kept, come))
    come = lax.ppermute(send, NAMES, pairs(1))
    packed = lax.all_to_all(copies, NAMES, 0, 0, axis_index_groups=planes(GATHER))
    (root,) = call(root_kernel, [((B, B), BF)], (packed,), flops=2 * 5 * B * B * B)
    (product,) = call(apply_kernel, [((2, 2, 2 * ROWS, B), BF)], (root, kept, come), flops=2 * 8 * ROWS * B * B)
    product = lax.all_to_all(product.reshape(8, ROWS, B), NAMES, 0, 0, axis_index_groups=groups())
    product = jnp.concatenate([product[2 * (yh ^ RETURN) :][:2] for yh in range(4)], axis=0)
    return product.transpose(1, 0, 2).reshape(ROWS, 8 * B)


def solution(mesh):
    names, sizes = zip(*AXES)
    cut = Mesh(mesh.devices.reshape(sizes), names)
    dp = names[:4]
    placed = (P(dp, "yh"), P(dp), P(names, None))
    return jax.shard_map(local, mesh=cut, in_specs=placed, out_specs=P(names, None), check_vma=False)
```

```python
import itertools

import jax
import jax.numpy as jnp
from jax import lax
from jax.experimental import pallas as pl
from jax.experimental.pallas import tpu as pltpu
from jax.sharding import Mesh, PartitionSpec as P

B = 512
H = 256
LANES = 128
DAMPING = 0.05
BF = jnp.bfloat16
F32 = jnp.float32
AXES = (("z", 8), ("yl", 2), ("x", 4), ("core", 2), ("yh", 4))
NAMES = tuple(name for name, _ in AXES)
SHARDS = 8
BELOW = [(row, column) for column in range(4) for row in range(column + 1, 4)]
PIECES = len(BELOW) + 3
PACKED = PIECES * LANES // SHARDS
HALF = LANES // 2
ROWS = 32
TOKENS = 512
MASK_ROWS = 16
ZFIRST = 6
SCATTER = 6
GATHER = 1
RETURN = 2
SLAB = TOKENS + 4 * ROWS + MASK_ROWS
VMEM_MIB = 16
VMEM = pl.BlockSpec(memory_space=pltpu.VMEM)
HBM = pl.BlockSpec(memory_space=pltpu.HBM)


def place(z, yl, x, core, yh):
    return (((z * 2 + yl) * 4 + x) * 2 + core) * 4 + yh


def groups():
    orders = [k ^ RETURN for k in range(4)]
    every = [(z, w, x) for z in range(8) for w in range(2) for x in range(4)]
    return [[place(z, w ^ (yh >> 1), x, core, yh) for yh in orders for core in range(2)] for z, w, x in every]


def layers():
    order = (ZFIRST, *[z for z in range(8) if z != ZFIRST])
    rests = itertools.product(range(2), range(4), range(2), range(4))
    return [[place(z, *rest) for z in order] for rest in rests]


def planes(first):
    spots = [divmod(k ^ first, 4) for k in range(SHARDS)]
    return [[place(z, yl, x, core, yh) for yl, x in spots] for z in range(8) for core in range(2) for yh in range(4)]


def pairs(flip):
    ends = [(2 * yh + core, 2 * (yh ^ flip) + core) for yh in range(4) for core in range(2)]
    return [(group[source], group[target]) for group in groups() for source, target in ends]


def call(kernel, outs, operands, specs=None, scratch=(), flops=0):
    shapes = [jax.ShapeDtypeStruct(*out) for out in outs]
    moved = sum(o.size * o.dtype.itemsize for o in (*operands, *shapes))
    return pl.pallas_call(
        kernel,
        out_shape=shapes,
        in_specs=specs or [VMEM] * len(operands),
        out_specs=[VMEM] * len(outs),
        scratch_shapes=scratch,
        cost_estimate=pl.CostEstimate(flops=flops, bytes_accessed=moved, transcendentals=0),
        compiler_params=pltpu.CompilerParams(vmem_limit_bytes=VMEM_MIB * 1024 * 1024),
    )(*operands)


def at(index, size=B):
    return pl.ds(pl.multiple_of(index * size, size), size)


def slab_kernel(act_ref, mask_ref, grad_ref, out_ref, mine_ref, mask_held, sems):
    other = 1 - lax.axis_index("core")
    copies = [pltpu.make_async_copy(act_ref.at[:, at(other)], out_ref.at[pl.ds(0, TOKENS)], sems.at[0])]
    for k in range(4):
        rows = pl.ds(TOKENS + ROWS * k, ROWS)
        copies.append(pltpu.make_async_copy(grad_ref.at[:, at(2 * k + other)], out_ref.at[rows], sems.at[k + 1]))
        rows = pl.ds(ROWS * k, ROWS)
        copies.append(pltpu.make_async_copy(grad_ref.at[:, at(2 * k + 1 - other)], mine_ref.at[rows], sems.at[k + 6]))
    copies.insert(0, pltpu.make_async_copy(mask_ref, mask_held, sems.at[5]))
    for copy in copies:
        copy.start()
    copies.pop(0).wait()
    mask = mask_held[...].astype(F32).astype(BF)
    out_ref[pl.ds(TOKENS + 4 * ROWS, MASK_ROWS), :] = jnp.broadcast_to(mask, (MASK_ROWS, TOKENS))
    for copy in copies:
        copy.wait()


def masked(columns, mask):
    column = jnp.broadcast_to(mask.astype(F32), (LANES, TOKENS)).T.astype(BF)
    return columns * jnp.concatenate([column] * (B // LANES), axis=1)


def triangle(columns):
    dot = lambda a, b: lax.dot_general(a, b, (((0,), (0,)), ((), ())), preferred_element_type=F32)
    low, high = columns[:, :H], columns[:, H:]
    return dot(low, low), dot(high, low), dot(high, high)


def own_kernel(act_ref, mask_ref, out_ref, held, mask_held, sems):
    columns = pltpu.make_async_copy(act_ref.at[:, at(lax.axis_index("core"))], held, sems.at[0])
    mask = pltpu.make_async_copy(mask_ref, mask_held, sems.at[1])
    columns.start()
    mask.start()
    columns.wait()
    mask.wait()
    for slot, block in enumerate(triangle(masked(held[...], mask_held[...]))):
        out_ref[slot] = block


def gram_kernel(slab_ref, own_ref, out_ref):
    mask = slab_ref[pl.ds(TOKENS + 4 * ROWS, MASK_ROWS), :][:1]
    blocks = triangle(masked(slab_ref[pl.ds(0, TOKENS), :], mask))
    blocks = [block + own_ref[slot] for slot, block in enumerate(blocks)]
    def cut(row, column):
        block = blocks[row // 2 + column // 2]
        row, column = LANES * (row % 2), LANES * (column % 2)
        return block[row : row + LANES, column : column + LANES]

    for piece, spot in enumerate(BELOW):
        out_ref[piece] = cut(*spot).astype(BF)
    left = lax.broadcasted_iota(jnp.int32, (HALF, LANES), 1) < HALF
    for pair in range(2):
        first, second = cut(2 * pair, 2 * pair), cut(2 * pair + 1, 2 * pair + 1)
        shared = jnp.where(left, second[:HALF], first[HALF:])
        out_ref[len(BELOW) + pair] = jnp.concatenate([first[:HALF], shared], axis=0).astype(BF)
        out_ref[len(BELOW) + 2, pl.ds(HALF * pair, HALF)] = second[HALF:].astype(BF)


def spread(parts_ref, out_ref):
    total = parts_ref[0].astype(F32)
    for part in range(1, SHARDS):
        total += parts_ref[part].astype(F32)
    rounded = total.astype(BF)
    for copy in range(SHARDS):
        out_ref[copy] = rounded


def first_sum(parts_ref, slab_ref, mine_ref, out_ref, send_ref, keep_ref):
    spread(parts_ref, out_ref)
    core, upper = lax.axis_index("core"), lax.axis_index("yh") // 2
    for ref, part in ((send_ref, 1 - upper), (keep_ref, upper)):
        for k in range(2):
            ref[k, core] = mine_ref[at(2 * part + k, ROWS), :]
            ref[k, 1 - core] = slab_ref[pl.ds(pl.multiple_of(TOKENS + ROWS * (2 * part + k), ROWS), ROWS), :]


def sum_kernel(parts_ref, kept_ref, come_ref, out_ref, send_ref, keep_ref):
    spread(parts_ref, out_ref)
    upper, lower = lax.axis_index("yh") // 2, lax.axis_index("yh") % 2
    for ref, part in ((send_ref, 1 - lower), (keep_ref, lower)):
        ref[upper] = kept_ref[part]
        ref[1 - upper] = come_ref[part]


def root_kernel(gram_ref, out_ref):
    shards = [gram_ref[spot ^ SCATTER ^ GATHER] for spot in range(SHARDS)]
    packed = jnp.concatenate(shards, axis=0).astype(F32)
    take = lambda row, count: packed[row : row + count]
    pieces = {spot: take(LANES * piece, LANES) for piece, spot in enumerate(BELOW)}
    row = lax.broadcasted_iota(jnp.int32, (LANES, LANES), 0)
    column = lax.broadcasted_iota(jnp.int32, (LANES, LANES), 1)
    for pair in range(2):
        base = LANES * (len(BELOW) + pair)
        first = take(base, LANES)
        second = jnp.concatenate([take(base + HALF, HALF), take(LANES * (len(BELOW) + 2) + HALF * pair, HALF)], axis=0)
        pieces[2 * pair, 2 * pair] = jnp.where((row >= HALF) & (column < HALF), first.T, first)
        pieces[2 * pair + 1, 2 * pair + 1] = jnp.where((row < HALF) & (column >= HALF), second.T, second)
    entry = lambda row, column: pieces[row, column] if row >= column else pieces[column, row].T
    gram = jnp.concatenate(
        [jnp.concatenate([entry(row, column) for column in range(4)], axis=1) for row in range(4)], axis=0
    )
    row = lax.broadcasted_iota(jnp.int32, (B, B), 0)
    column = lax.broadcasted_iota(jnp.int32, (B, B), 1)
    identity = jnp.where(row == column, 1.0, 0.0).astype(F32)
    damped = gram * (1.0 / 65536) + DAMPING * identity
    norm = jnp.max(jnp.sum(jnp.abs(damped), axis=1, keepdims=True), axis=0, keepdims=True)
    dot = lambda left, right: jnp.dot(left, right, preferred_element_type=F32)
    y = damped * (1.0 / norm)
    near = y.astype(BF)
    square = dot(near, near)
    z = 2.25 * identity - 2.4375 * y + 1.6875 * square + dot(square.astype(BF), (0.0625 * square - 0.5625 * y).astype(BF))
    close = z.astype(BF)
    both = dot(jnp.concatenate([close, near], axis=0), close).astype(BF)
    root = 1.5 * z - 0.5 * dot(both[:B], both[B:])
    out_ref[...] = (root * (1.0 / jnp.sqrt(norm))).astype(BF)


def apply_kernel(root_ref, kept_ref, come_ref, out_ref):
    turn = lax.axis_index("yh") // 2 + lax.axis_index("yh") % 2
    for ref, other in ((kept_ref, 0), (come_ref, 1)):
        product = jnp.dot(ref[...].reshape(4 * ROWS, B), root_ref[...], preferred_element_type=F32).astype(BF)
        for upper in range(2):
            out_ref[upper ^ (RETURN >> 1), (turn + upper + other + RETURN) % 2] = product[2 * ROWS * upper : 2 * ROWS * (upper + 1)]


def local(activations, token_mask, gradient):
    mask = pltpu.with_memory_space_constraint(token_mask.reshape(1, TOKENS), pltpu.HBM)
    activations = pltpu.with_memory_space_constraint(activations, pltpu.HBM)
    gradient = pltpu.with_memory_space_constraint(gradient, pltpu.HBM)
    dma = pltpu.SemaphoreType.DMA
    slab, mine = call(
        slab_kernel,
        [((SLAB, B), BF), ((4 * ROWS, B), BF)],
        (activations, mask, gradient),
        [HBM] * 3,
        [pltpu.VMEM((1, TOKENS), jnp.int32), dma((10,))],
    )
    other = lax.ppermute(slab, "core", [(0, 1), (1, 0)])
    (own,) = call(
        own_kernel,
        [((3, H, H), F32)],
        (activations, mask),
        [HBM, HBM],
        [pltpu.VMEM((TOKENS, B), BF), pltpu.VMEM((1, TOKENS), jnp.int32), dma((2,))],
        flops=6 * TOKENS * H * H,
    )
    half = ((2, 2, ROWS, B), BF)
    (packed,) = call(gram_kernel, [((PIECES, LANES, LANES), BF)], (other, own), flops=6 * TOKENS * H * H)
    parts = lax.all_to_all(packed.reshape(SHARDS, PACKED, LANES), NAMES, 0, 0, axis_index_groups=planes(SCATTER))
    copies, send, kept = call(first_sum, [(parts.shape, BF), half, half], (parts, other, mine))
    come = lax.ppermute(send, NAMES, pairs(3))
    parts = lax.all_to_all(copies, NAMES, 0, 0, axis_index_groups=layers())
    copies, send, kept = call(sum_kernel, [(parts.shape, BF), half, half], (parts, kept, come))
    come = lax.ppermute(send, NAMES, pairs(1))
    packed = lax.all_to_all(copies, NAMES, 0, 0, axis_index_groups=planes(GATHER))
    (root,) = call(root_kernel, [((B, B), BF)], (packed,), flops=2 * 5 * B * B * B)
    (product,) = call(apply_kernel, [((2, 2, 2 * ROWS, B), BF)], (root, kept, come), flops=2 * 8 * ROWS * B * B)
    product = lax.all_to_all(product.reshape(8, ROWS, B), NAMES, 0, 0, axis_index_groups=groups())
    product = jnp.concatenate([product[2 * (yh ^ RETURN) :][:2] for yh in range(4)], axis=0)
    return product.transpose(1, 0, 2).reshape(ROWS, 8 * B)


def solution(mesh):
    names, sizes = zip(*AXES)
    cut = Mesh(mesh.devices.reshape(sizes), names)
    dp = names[:4]
    placed = (P(dp, "yh"), P(dp), P(names, None))
    return jax.shard_map(local, mesh=cut, in_specs=placed, out_specs=P(names, None), check_vma=False)
```

```python
import jax
import jax.numpy as jnp
from jax import lax
from jax.experimental import pallas as pl
from jax.experimental.pallas import tpu as pltpu
from jax.sharding import Mesh, PartitionSpec as P

B = 512
H = 256
LANES = 128
DAMPING = 0.05
BF = jnp.bfloat16
F32 = jnp.float32
AXES = (("z", 8), ("yl", 2), ("x", 4), ("core", 2), ("yh", 4))
NAMES = tuple(name for name, _ in AXES)
SHARDS = 8
BELOW = [(row, column) for column in range(4) for row in range(column + 1, 4)]
PIECES = len(BELOW) + 3
PACKED = PIECES * LANES // SHARDS
HALF = LANES // 2
ROWS = 32
TOKENS = 512
MASK_ROWS = 16
SCATTER = 6
GATHER = 4
RETURN = 2
FIRST = 3
SECOND = 1
SLAB = TOKENS + 4 * ROWS + MASK_ROWS
VMEM_MIB = 16
VMEM = pl.BlockSpec(memory_space=pltpu.VMEM)
HBM = pl.BlockSpec(memory_space=pltpu.HBM)


def place(z, yl, x, core, yh):
    return (((z * 2 + yl) * 4 + x) * 2 + core) * 4 + yh


def groups():
    orders = [k ^ RETURN for k in range(4)]
    every = [(z, w, x) for z in range(8) for w in range(2) for x in range(4)]
    return [[place(z, w ^ (yh >> 1), x, core, yh) for yh in orders for core in range(2)] for z, w, x in every]


def planes(first):
    spots = [divmod(k ^ first, 4) for k in range(SHARDS)]
    return [[place(z, yl, x, core, yh) for yl, x in spots] for z in range(8) for core in range(2) for yh in range(4)]


def pairs(flip):
    ends = [(2 * yh + core, 2 * (yh ^ flip) + core) for yh in range(4) for core in range(2)]
    return [(group[source], group[target]) for group in groups() for source, target in ends]


def call(kernel, outs, operands, specs=None, scratch=(), flops=0):
    shapes = [jax.ShapeDtypeStruct(*out) for out in outs]
    moved = sum(o.size * o.dtype.itemsize for o in (*operands, *shapes))
    return pl.pallas_call(
        kernel,
        out_shape=shapes,
        in_specs=specs or [VMEM] * len(operands),
        out_specs=[VMEM] * len(outs),
        scratch_shapes=scratch,
        cost_estimate=pl.CostEstimate(flops=flops, bytes_accessed=moved, transcendentals=0),
        compiler_params=pltpu.CompilerParams(vmem_limit_bytes=VMEM_MIB * 1024 * 1024),
    )(*operands)


def at(index, size=B):
    return pl.ds(pl.multiple_of(index * size, size), size)


def slab_kernel(act_ref, mask_ref, grad_ref, out_ref, mine_ref, mask_held, sems):
    other = 1 - lax.axis_index("core")
    copies = [pltpu.make_async_copy(act_ref.at[:, at(other)], out_ref.at[pl.ds(0, TOKENS)], sems.at[0])]
    for k in range(4):
        rows = pl.ds(TOKENS + ROWS * k, ROWS)
        copies.append(pltpu.make_async_copy(grad_ref.at[:, at(2 * k + other)], out_ref.at[rows], sems.at[k + 1]))
        rows = pl.ds(ROWS * k, ROWS)
        copies.append(pltpu.make_async_copy(grad_ref.at[:, at(2 * k + 1 - other)], mine_ref.at[rows], sems.at[k + 6]))
    copies.insert(0, pltpu.make_async_copy(mask_ref, mask_held, sems.at[5]))
    for copy in copies:
        copy.start()
    copies.pop(0).wait()
    mask = mask_held[...].astype(F32).astype(BF)
    out_ref[pl.ds(TOKENS + 4 * ROWS, MASK_ROWS), :] = jnp.broadcast_to(mask, (MASK_ROWS, TOKENS))
    for copy in copies:
        copy.wait()


def masked(columns, mask):
    column = jnp.broadcast_to(mask.astype(F32), (LANES, TOKENS)).T.astype(BF)
    return columns * jnp.concatenate([column] * (B // LANES), axis=1)


def triangle(columns):
    dot = lambda a, b: lax.dot_general(a, b, (((0,), (0,)), ((), ())), preferred_element_type=F32)
    low, high = columns[:, :H], columns[:, H:]
    return dot(low, low), dot(high, low), dot(high, high)


def own_kernel(act_ref, mask_ref, out_ref, held, mask_held, sems):
    columns = pltpu.make_async_copy(act_ref.at[:, at(lax.axis_index("core"))], held, sems.at[0])
    mask = pltpu.make_async_copy(mask_ref, mask_held, sems.at[1])
    columns.start()
    mask.start()
    columns.wait()
    mask.wait()
    for slot, block in enumerate(triangle(masked(held[...], mask_held[...]))):
        out_ref[slot] = block


def gram_kernel(slab_ref, own_ref, out_ref):
    mask = slab_ref[pl.ds(TOKENS + 4 * ROWS, MASK_ROWS), :][:1]
    blocks = triangle(masked(slab_ref[pl.ds(0, TOKENS), :], mask))
    blocks = [block + own_ref[slot] for slot, block in enumerate(blocks)]
    def cut(row, column):
        block = blocks[row // 2 + column // 2]
        row, column = LANES * (row % 2), LANES * (column % 2)
        return block[row : row + LANES, column : column + LANES]

    for piece, spot in enumerate(BELOW):
        out_ref[piece] = cut(*spot).astype(BF)
    left = lax.broadcasted_iota(jnp.int32, (HALF, LANES), 1) < HALF
    for pair in range(2):
        first, second = cut(2 * pair, 2 * pair), cut(2 * pair + 1, 2 * pair + 1)
        shared = jnp.where(left, second[:HALF], first[HALF:])
        out_ref[len(BELOW) + pair] = jnp.concatenate([first[:HALF], shared], axis=0).astype(BF)
        out_ref[len(BELOW) + 2, pl.ds(HALF * pair, HALF)] = second[HALF:].astype(BF)


def spread(parts_ref, out_ref):
    total = parts_ref[0].astype(F32)
    for part in range(1, SHARDS):
        total += parts_ref[part].astype(F32)
    rounded = total.astype(BF)
    for copy in range(SHARDS):
        out_ref[copy] = rounded


def first_sum(parts_ref, slab_ref, mine_ref, out_ref, send_ref, keep_ref):
    spread(parts_ref, out_ref)
    core, upper = lax.axis_index("core"), lax.axis_index("yh") // 2
    for ref, part in ((send_ref, 1 - upper), (keep_ref, upper)):
        for k in range(2):
            ref[k, core] = mine_ref[at(2 * part + k, ROWS), :]
            ref[k, 1 - core] = slab_ref[pl.ds(pl.multiple_of(TOKENS + ROWS * (2 * part + k), ROWS), ROWS), :]


def first_sum(parts_ref, slab_ref, mine_ref, out_ref, send_ref, keep_ref):
    spread(parts_ref, out_ref)
    core, tensor = lax.axis_index("core"), lax.axis_index("yh")
    for ref, flip in ((send_ref, FIRST), (keep_ref, 0)):
        for k in range(2):
            owner = tensor ^ flip ^ (SECOND * k)
            ref[k, core] = mine_ref[at(owner, ROWS), :]
            ref[k, 1 - core] = slab_ref[pl.ds(pl.multiple_of(TOKENS + ROWS * owner, ROWS), ROWS), :]


def sum_kernel(parts_ref, kept_ref, come_ref, out_ref, send_ref, keep_ref):
    spread(parts_ref, out_ref)
    for k, ref in enumerate((keep_ref, send_ref)):
        ref[0] = kept_ref[k]
        ref[1] = come_ref[k]


def root_kernel(gram_ref, out_ref):
    shards = [gram_ref[spot ^ SCATTER ^ GATHER] for spot in range(SHARDS)]
    packed = jnp.concatenate(shards, axis=0).astype(F32)
    take = lambda row, count: packed[row : row + count]
    pieces = {spot: take(LANES * piece, LANES) for piece, spot in enumerate(BELOW)}
    row = lax.broadcasted_iota(jnp.int32, (LANES, LANES), 0)
    column = lax.broadcasted_iota(jnp.int32, (LANES, LANES), 1)
    for pair in range(2):
        base = LANES * (len(BELOW) + pair)
        first = take(base, LANES)
        second = jnp.concatenate([take(base + HALF, HALF), take(LANES * (len(BELOW) + 2) + HALF * pair, HALF)], axis=0)
        pieces[2 * pair, 2 * pair] = jnp.where((row >= HALF) & (column < HALF), first.T, first)
        pieces[2 * pair + 1, 2 * pair + 1] = jnp.where((row < HALF) & (column >= HALF), second.T, second)
    entry = lambda row, column: pieces[row, column] if row >= column else pieces[column, row].T
    gram = jnp.concatenate(
        [jnp.concatenate([entry(row, column) for column in range(4)], axis=1) for row in range(4)], axis=0
    )
    row = lax.broadcasted_iota(jnp.int32, (B, B), 0)
    column = lax.broadcasted_iota(jnp.int32, (B, B), 1)
    identity = jnp.where(row == column, 1.0, 0.0).astype(F32)
    damped = gram * (1.0 / 65536) + DAMPING * identity
    norm = jnp.max(jnp.sum(jnp.abs(damped), axis=1, keepdims=True), axis=0, keepdims=True)
    dot = lambda left, right: jnp.dot(left, right, preferred_element_type=F32)
    y = damped * (1.0 / norm)
    near = y.astype(BF)
    square = dot(near, near)
    z = 2.25 * identity - 2.4375 * y + 1.6875 * square + dot(square.astype(BF), (0.0625 * square - 0.5625 * y).astype(BF))
    close = z.astype(BF)
    both = dot(jnp.concatenate([close, near], axis=0), close).astype(BF)
    root = 1.5 * z - 0.5 * dot(both[:B], both[B:])
    out_ref[...] = (root * (1.0 / jnp.sqrt(norm))).astype(BF)


def apply_kernel(root_ref, kept_ref, come_ref, out_ref):
    spot = lax.axis_index("yh") ^ RETURN
    for ref, flip in ((kept_ref, 0), (come_ref, SECOND)):
        product = jnp.dot(ref[...].reshape(4 * ROWS, B), root_ref[...], preferred_element_type=F32).astype(BF)
        for k in range(2):
            out_ref[spot ^ flip ^ (FIRST * k)] = product[2 * ROWS * k : 2 * ROWS * (k + 1)]


def local(activations, token_mask, gradient):
    mask = pltpu.with_memory_space_constraint(token_mask.reshape(1, TOKENS), pltpu.HBM)
    activations = pltpu.with_memory_space_constraint(activations, pltpu.HBM)
    gradient = pltpu.with_memory_space_constraint(gradient, pltpu.HBM)
    dma = pltpu.SemaphoreType.DMA
    slab, mine = call(
        slab_kernel,
        [((SLAB, B), BF), ((4 * ROWS, B), BF)],
        (activations, mask, gradient),
        [HBM] * 3,
        [pltpu.VMEM((1, TOKENS), jnp.int32), dma((10,))],
    )
    other = lax.ppermute(slab, "core", [(0, 1), (1, 0)])
    (own,) = call(
        own_kernel,
        [((3, H, H), F32)],
        (activations, mask),
        [HBM, HBM],
        [pltpu.VMEM((TOKENS, B), BF), pltpu.VMEM((1, TOKENS), jnp.int32), dma((2,))],
        flops=6 * TOKENS * H * H,
    )
    half = ((2, 2, ROWS, B), BF)
    (packed,) = call(gram_kernel, [((PIECES, LANES, LANES), BF)], (other, own), flops=6 * TOKENS * H * H)
    parts = lax.all_to_all(packed.reshape(SHARDS, PACKED, LANES), NAMES, 0, 0, axis_index_groups=planes(SCATTER))
    copies, send, kept = call(first_sum, [(parts.shape, BF), half, half], (parts, other, mine))
    come = lax.ppermute(send, NAMES, pairs(FIRST))
    parts = lax.all_to_all(copies, "z", 0, 0)
    copies, send, kept = call(sum_kernel, [(parts.shape, BF), half, half], (parts, kept, come))
    come = lax.ppermute(send, NAMES, pairs(SECOND))
    packed = lax.all_to_all(copies, NAMES, 0, 0, axis_index_groups=planes(GATHER))
    (root,) = call(root_kernel, [((B, B), BF)], (packed,), flops=2 * 5 * B * B * B)
    (product,) = call(apply_kernel, [((4, 2 * ROWS, B), BF)], (root, kept, come), flops=2 * 8 * ROWS * B * B)
    product = lax.all_to_all(product.reshape(8, ROWS, B), NAMES, 0, 0, axis_index_groups=groups())
    product = jnp.concatenate([product[2 * (yh ^ RETURN) :][:2] for yh in range(4)], axis=0)
    return product.transpose(1, 0, 2).reshape(ROWS, 8 * B)


def solution(mesh):
    names, sizes = zip(*AXES)
    cut = Mesh(mesh.devices.reshape(sizes), names)
    dp = names[:4]
    placed = (P(dp, "yh"), P(dp), P(names, None))
    return jax.shard_map(local, mesh=cut, in_specs=placed, out_specs=P(names, None), check_vma=False)
```

```python
import jax
import jax.numpy as jnp
from jax import lax
from jax.experimental import pallas as pl
from jax.experimental.pallas import tpu as pltpu
from jax.sharding import Mesh, PartitionSpec as P

B = 512
H = 256
LANES = 128
DAMPING = 0.05
BF = jnp.bfloat16
F32 = jnp.float32
AXES = (("z", 8), ("yl", 2), ("x", 4), ("core", 2), ("yh", 4))
NAMES = tuple(name for name, _ in AXES)
SHARDS = 8
BELOW = [(row, column) for column in range(4) for row in range(column + 1, 4)]
PIECES = len(BELOW) + 3
PACKED = PIECES * LANES // SHARDS
HALF = LANES // 2
ROWS = 32
TOKENS = 512
MASK_ROWS = 16
SCATTER = 6
GATHER = 4
RETURN = 2
FIRST = 3
SECOND = 1
SLAB = TOKENS + 4 * ROWS + MASK_ROWS
VMEM_MIB = 16
VMEM = pl.BlockSpec(memory_space=pltpu.VMEM)
HBM = pl.BlockSpec(memory_space=pltpu.HBM)


def place(z, yl, x, core, yh):
    return (((z * 2 + yl) * 4 + x) * 2 + core) * 4 + yh


def groups():
    orders = [k ^ RETURN for k in range(4)]
    every = [(z, w, x) for z in range(8) for w in range(2) for x in range(4)]
    return [[place(z, w ^ (yh >> 1), x, core, yh) for yh in orders for core in range(2)] for z, w, x in every]


def planes(first):
    spots = [divmod(k ^ first, 4) for k in range(SHARDS)]
    return [[place(z, yl, x, core, yh) for yl, x in spots] for z in range(8) for core in range(2) for yh in range(4)]


def pairs(flip):
    ends = [(2 * yh + core, 2 * (yh ^ flip) + core) for yh in range(4) for core in range(2)]
    return [(group[source], group[target]) for group in groups() for source, target in ends]


def call(kernel, outs, operands, specs=None, scratch=(), flops=0):
    shapes = [jax.ShapeDtypeStruct(*out) for out in outs]
    moved = sum(o.size * o.dtype.itemsize for o in (*operands, *shapes))
    return pl.pallas_call(
        kernel,
        out_shape=shapes,
        in_specs=specs or [VMEM] * len(operands),
        out_specs=[VMEM] * len(outs),
        scratch_shapes=scratch,
        cost_estimate=pl.CostEstimate(flops=flops, bytes_accessed=moved, transcendentals=0),
        compiler_params=pltpu.CompilerParams(vmem_limit_bytes=VMEM_MIB * 1024 * 1024),
    )(*operands)


def at(index, size=B):
    return pl.ds(pl.multiple_of(index * size, size), size)


def slab_kernel(act_ref, mask_ref, grad_ref, out_ref, mine_ref, mask_held, sems):
    other = 1 - lax.axis_index("core")
    copies = [pltpu.make_async_copy(act_ref.at[:, at(other)], out_ref.at[pl.ds(0, TOKENS)], sems.at[0])]
    for k in range(4):
        rows = pl.ds(TOKENS + ROWS * k, ROWS)
        copies.append(pltpu.make_async_copy(grad_ref.at[:, at(2 * k + other)], out_ref.at[rows], sems.at[k + 1]))
        rows = pl.ds(ROWS * k, ROWS)
        copies.append(pltpu.make_async_copy(grad_ref.at[:, at(2 * k + 1 - other)], mine_ref.at[rows], sems.at[k + 6]))
    copies.insert(0, pltpu.make_async_copy(mask_ref, mask_held, sems.at[5]))
    for copy in copies:
        copy.start()
    copies.pop(0).wait()
    mask = mask_held[...].astype(F32).astype(BF)
    out_ref[pl.ds(TOKENS + 4 * ROWS, MASK_ROWS), :] = jnp.broadcast_to(mask, (MASK_ROWS, TOKENS))
    for copy in copies:
        copy.wait()


def masked(columns, mask):
    column = jnp.broadcast_to(mask.astype(F32), (LANES, TOKENS)).T.astype(BF)
    return columns * jnp.concatenate([column] * (B // LANES), axis=1)


def triangle(columns):
    dot = lambda a, b: lax.dot_general(a, b, (((0,), (0,)), ((), ())), preferred_element_type=F32)
    low, high = columns[:, :H], columns[:, H:]
    return dot(low, low), dot(high, low), dot(high, high)


def own_kernel(act_ref, mask_ref, out_ref, held, mask_held, sems):
    columns = pltpu.make_async_copy(act_ref.at[:, at(lax.axis_index("core"))], held, sems.at[0])
    mask = pltpu.make_async_copy(mask_ref, mask_held, sems.at[1])
    columns.start()
    mask.start()
    columns.wait()
    mask.wait()
    for slot, block in enumerate(triangle(masked(held[...], mask_held[...]))):
        out_ref[slot] = block


def gram_kernel(slab_ref, own_ref, out_ref):
    mask = slab_ref[pl.ds(TOKENS + 4 * ROWS, MASK_ROWS), :][:1]
    blocks = triangle(masked(slab_ref[pl.ds(0, TOKENS), :], mask))
    blocks = [block + own_ref[slot] for slot, block in enumerate(blocks)]
    def cut(row, column):
        block = blocks[row // 2 + column // 2]
        row, column = LANES * (row % 2), LANES * (column % 2)
        return block[row : row + LANES, column : column + LANES]

    for piece, spot in enumerate(BELOW):
        out_ref[piece] = cut(*spot).astype(BF)
    left = lax.broadcasted_iota(jnp.int32, (HALF, LANES), 1) < HALF
    for pair in range(2):
        first, second = cut(2 * pair, 2 * pair), cut(2 * pair + 1, 2 * pair + 1)
        shared = jnp.where(left, second[:HALF], first[HALF:])
        out_ref[len(BELOW) + pair] = jnp.concatenate([first[:HALF], shared], axis=0).astype(BF)
        out_ref[len(BELOW) + 2, pl.ds(HALF * pair, HALF)] = second[HALF:].astype(BF)


def spread(parts_ref, out_ref):
    total = parts_ref[0].astype(F32)
    for part in range(1, SHARDS):
        total += parts_ref[part].astype(F32)
    rounded = total.astype(BF)
    for copy in range(SHARDS):
        out_ref[copy] = rounded


def first_sum(parts_ref, slab_ref, mine_ref, out_ref, send_ref, keep_ref):
    spread(parts_ref, out_ref)
    core, tensor = lax.axis_index("core"), lax.axis_index("yh")
    for ref, flip in ((send_ref, FIRST), (keep_ref, 0)):
        for k in range(2):
            owner = tensor ^ flip ^ (SECOND * k)
            ref[k, core] = mine_ref[at(owner, ROWS), :]
            ref[k, 1 - core] = slab_ref[pl.ds(pl.multiple_of(TOKENS + ROWS * owner, ROWS), ROWS), :]


def sum_kernel(parts_ref, kept_ref, come_ref, out_ref, send_ref, keep_ref):
    spread(parts_ref, out_ref)
    for k, ref in enumerate((keep_ref, send_ref)):
        ref[0] = kept_ref[k]
        ref[1] = come_ref[k]


def root_kernel(gram_ref, kept_ref, out_ref, product_ref):
    shards = [gram_ref[spot ^ SCATTER ^ GATHER] for spot in range(SHARDS)]
    packed = jnp.concatenate(shards, axis=0).astype(F32)
    take = lambda row, count: packed[row : row + count]
    pieces = {spot: take(LANES * piece, LANES) for piece, spot in enumerate(BELOW)}
    row = lax.broadcasted_iota(jnp.int32, (LANES, LANES), 0)
    column = lax.broadcasted_iota(jnp.int32, (LANES, LANES), 1)
    for pair in range(2):
        base = LANES * (len(BELOW) + pair)
        first = take(base, LANES)
        second = jnp.concatenate([take(base + HALF, HALF), take(LANES * (len(BELOW) + 2) + HALF * pair, HALF)], axis=0)
        pieces[2 * pair, 2 * pair] = jnp.where((row >= HALF) & (column < HALF), first.T, first)
        pieces[2 * pair + 1, 2 * pair + 1] = jnp.where((row < HALF) & (column >= HALF), second.T, second)
    entry = lambda row, column: pieces[row, column] if row >= column else pieces[column, row].T
    gram = jnp.concatenate(
        [jnp.concatenate([entry(row, column) for column in range(4)], axis=1) for row in range(4)], axis=0
    )
    row = lax.broadcasted_iota(jnp.int32, (B, B), 0)
    column = lax.broadcasted_iota(jnp.int32, (B, B), 1)
    identity = jnp.where(row == column, 1.0, 0.0).astype(F32)
    damped = gram * (1.0 / 65536) + DAMPING * identity
    norm = jnp.max(jnp.sum(jnp.abs(damped), axis=1, keepdims=True), axis=0, keepdims=True)
    dot = lambda left, right: jnp.dot(left, right, preferred_element_type=F32)
    y = damped * (1.0 / norm)
    near = y.astype(BF)
    square = dot(near, near)
    z = 2.25 * identity - 2.4375 * y + 1.6875 * square + dot(square.astype(BF), (0.0625 * square - 0.5625 * y).astype(BF))
    close = z.astype(BF)
    both = dot(jnp.concatenate([close, near], axis=0), close).astype(BF)
    root = 1.5 * z - 0.5 * dot(both[:B], both[B:])
    root = (root * (1.0 / jnp.sqrt(norm))).astype(BF)
    out_ref[...] = root
    product_ref[...] = dot(kept_ref[...].reshape(4 * ROWS, B), root).astype(BF)


def apply_kernel(root_ref, product_ref, come_ref, out_ref):
    spot = lax.axis_index("yh") ^ RETURN
    late = jnp.dot(come_ref[...].reshape(4 * ROWS, B), root_ref[...], preferred_element_type=F32).astype(BF)
    for product, flip in ((product_ref[...], 0), (late, SECOND)):
        for k in range(2):
            out_ref[spot ^ flip ^ (FIRST * k)] = product[2 * ROWS * k : 2 * ROWS * (k + 1)]


def local(activations, token_mask, gradient):
    mask = pltpu.with_memory_space_constraint(token_mask.reshape(1, TOKENS), pltpu.HBM)
    activations = pltpu.with_memory_space_constraint(activations, pltpu.HBM)
    gradient = pltpu.with_memory_space_constraint(gradient, pltpu.HBM)
    dma = pltpu.SemaphoreType.DMA
    slab, mine = call(
        slab_kernel,
        [((SLAB, B), BF), ((4 * ROWS, B), BF)],
        (activations, mask, gradient),
        [HBM] * 3,
        [pltpu.VMEM((1, TOKENS), jnp.int32), dma((10,))],
    )
    other = lax.ppermute(slab, "core", [(0, 1), (1, 0)])
    (own,) = call(
        own_kernel,
        [((3, H, H), F32)],
        (activations, mask),
        [HBM, HBM],
        [pltpu.VMEM((TOKENS, B), BF), pltpu.VMEM((1, TOKENS), jnp.int32), dma((2,))],
        flops=6 * TOKENS * H * H,
    )
    half = ((2, 2, ROWS, B), BF)
    (packed,) = call(gram_kernel, [((PIECES, LANES, LANES), BF)], (other, own), flops=6 * TOKENS * H * H)
    parts = lax.all_to_all(packed.reshape(SHARDS, PACKED, LANES), NAMES, 0, 0, axis_index_groups=planes(SCATTER))
    copies, send, kept = call(first_sum, [(parts.shape, BF), half, half], (parts, other, mine))
    come = lax.ppermute(send, NAMES, pairs(FIRST))
    parts = lax.all_to_all(copies, "z", 0, 0)
    copies, send, kept = call(sum_kernel, [(parts.shape, BF), half, half], (parts, kept, come))
    come = lax.ppermute(send, NAMES, pairs(SECOND))
    packed = lax.all_to_all(copies, NAMES, 0, 0, axis_index_groups=planes(GATHER))
    root, product = call(
        root_kernel, [((B, B), BF), ((4 * ROWS, B), BF)], (packed, kept), flops=2 * 5 * B * B * B
    )
    (product,) = call(
        apply_kernel, [((4, 2 * ROWS, B), BF)], (root, product, come), flops=2 * 4 * ROWS * B * B
    )
    product = lax.all_to_all(product.reshape(8, ROWS, B), NAMES, 0, 0, axis_index_groups=groups())
    product = jnp.concatenate([product[2 * (yh ^ RETURN) :][:2] for yh in range(4)], axis=0)
    return product.transpose(1, 0, 2).reshape(ROWS, 8 * B)


def solution(mesh):
    names, sizes = zip(*AXES)
    cut = Mesh(mesh.devices.reshape(sizes), names)
    dp = names[:4]
    placed = (P(dp, "yh"), P(dp), P(names, None))
    return jax.shard_map(local, mesh=cut, in_specs=placed, out_specs=P(names, None), check_vma=False)
```

```python
import jax
import jax.numpy as jnp
from jax import lax
from jax.experimental import pallas as pl
from jax.experimental.pallas import tpu as pltpu
from jax.sharding import Mesh, PartitionSpec as P

B = 512
H = 256
LANES = 128
DAMPING = 0.05
BF = jnp.bfloat16
F32 = jnp.float32
AXES = (("z", 8), ("yl", 2), ("x", 4), ("core", 2), ("yh", 4))
NAMES = tuple(name for name, _ in AXES)
SHARDS = 8
BELOW = [(row, column) for column in range(4) for row in range(column + 1, 4)]
PIECES = len(BELOW) + 3
PACKED = PIECES * LANES // SHARDS
HALF = LANES // 2
ROWS = 32
TOKENS = 512
MASK_ROWS = 16
SCATTER = 6
GATHER = 4
RETURN = 2
FIRST = 3
SECOND = 1
SLAB = TOKENS + 4 * ROWS + MASK_ROWS
VMEM_MIB = 16
VMEM = pl.BlockSpec(memory_space=pltpu.VMEM)
HBM = pl.BlockSpec(memory_space=pltpu.HBM)


def place(z, yl, x, core, yh):
    return (((z * 2 + yl) * 4 + x) * 2 + core) * 4 + yh


def groups():
    orders = [k ^ RETURN for k in range(4)]
    every = [(z, w, x) for z in range(8) for w in range(2) for x in range(4)]
    return [[place(z, w ^ (yh >> 1), x, core, yh) for yh in orders for core in range(2)] for z, w, x in every]


def planes(first):
    spots = [divmod(k ^ first, 4) for k in range(SHARDS)]
    return [[place(z, yl, x, core, yh) for yl, x in spots] for z in range(8) for core in range(2) for yh in range(4)]


def pairs(flip):
    ends = [(2 * yh + core, 2 * (yh ^ flip) + core) for yh in range(4) for core in range(2)]
    return [(group[source], group[target]) for group in groups() for source, target in ends]


def call(kernel, outs, operands, specs=None, scratch=(), flops=0):
    shapes = [jax.ShapeDtypeStruct(*out) for out in outs]
    moved = sum(o.size * o.dtype.itemsize for o in (*operands, *shapes))
    return pl.pallas_call(
        kernel,
        out_shape=shapes,
        in_specs=specs or [VMEM] * len(operands),
        out_specs=[VMEM] * len(outs),
        scratch_shapes=scratch,
        cost_estimate=pl.CostEstimate(flops=flops, bytes_accessed=moved, transcendentals=0),
        compiler_params=pltpu.CompilerParams(vmem_limit_bytes=VMEM_MIB * 1024 * 1024),
    )(*operands)


def at(index, size=B):
    return pl.ds(pl.multiple_of(index * size, size), size)


def slab_kernel(act_ref, mask_ref, grad_ref, out_ref, mask_held, sems):
    other = 1 - lax.axis_index("core")
    copies = [pltpu.make_async_copy(act_ref.at[:, at(other)], out_ref.at[pl.ds(0, TOKENS)], sems.at[0])]
    for k in range(4):
        rows = pl.ds(TOKENS + ROWS * k, ROWS)
        copies.append(pltpu.make_async_copy(grad_ref.at[:, at(2 * k + other)], out_ref.at[rows], sems.at[k + 1]))
    copies.insert(0, pltpu.make_async_copy(mask_ref, mask_held, sems.at[5]))
    for copy in copies:
        copy.start()
    copies.pop(0).wait()
    mask = mask_held[...].astype(F32).astype(BF)
    out_ref[pl.ds(TOKENS + 4 * ROWS, MASK_ROWS), :] = jnp.broadcast_to(mask, (MASK_ROWS, TOKENS))
    for copy in copies:
        copy.wait()


def masked(columns, mask):
    column = jnp.broadcast_to(mask.astype(F32), (LANES, TOKENS)).T.astype(BF)
    return columns * jnp.concatenate([column] * (B // LANES), axis=1)


def triangle(columns):
    dot = lambda a, b: lax.dot_general(a, b, (((0,), (0,)), ((), ())), preferred_element_type=F32)
    low, high = columns[:, :H], columns[:, H:]
    return dot(low, low), dot(high, low), dot(high, high)


def own_kernel(act_ref, mask_ref, grad_ref, out_ref, mine_ref, held, mask_held, sems):
    core = lax.axis_index("core")
    copies = [pltpu.make_async_copy(act_ref.at[:, at(core)], held, sems.at[0])]
    copies.append(pltpu.make_async_copy(mask_ref, mask_held, sems.at[1]))
    for k in range(4):
        rows = pl.ds(ROWS * k, ROWS)
        copies.append(pltpu.make_async_copy(grad_ref.at[:, at(2 * k + core)], mine_ref.at[rows], sems.at[k + 2]))
    for copy in copies:
        copy.start()
    for copy in copies:
        copy.wait()
    for slot, block in enumerate(triangle(masked(held[...], mask_held[...]))):
        out_ref[slot] = block


def gram_kernel(slab_ref, own_ref, out_ref):
    mask = slab_ref[pl.ds(TOKENS + 4 * ROWS, MASK_ROWS), :][:1]
    blocks = triangle(masked(slab_ref[pl.ds(0, TOKENS), :], mask))
    blocks = [block + own_ref[slot] for slot, block in enumerate(blocks)]
    def cut(row, column):
        block = blocks[row // 2 + column // 2]
        row, column = LANES * (row % 2), LANES * (column % 2)
        return block[row : row + LANES, column : column + LANES]

    for piece, spot in enumerate(BELOW):
        out_ref[piece] = cut(*spot).astype(BF)
    left = lax.broadcasted_iota(jnp.int32, (HALF, LANES), 1) < HALF
    for pair in range(2):
        first, second = cut(2 * pair, 2 * pair), cut(2 * pair + 1, 2 * pair + 1)
        shared = jnp.where(left, second[:HALF], first[HALF:])
        out_ref[len(BELOW) + pair] = jnp.concatenate([first[:HALF], shared], axis=0).astype(BF)
        out_ref[len(BELOW) + 2, pl.ds(HALF * pair, HALF)] = second[HALF:].astype(BF)


def spread(parts_ref, out_ref):
    total = parts_ref[0].astype(F32)
    for part in range(1, SHARDS):
        total += parts_ref[part].astype(F32)
    rounded = total.astype(BF)
    for copy in range(SHARDS):
        out_ref[copy] = rounded


def first_sum(parts_ref, slab_ref, mine_ref, out_ref, send_ref, keep_ref):
    spread(parts_ref, out_ref)
    core, tensor = lax.axis_index("core"), lax.axis_index("yh")
    for ref, flip in ((send_ref, FIRST), (keep_ref, 0)):
        for k in range(2):
            owner = tensor ^ flip ^ (SECOND * k)
            ref[k, core] = mine_ref[at(owner, ROWS), :]
            ref[k, 1 - core] = slab_ref[pl.ds(pl.multiple_of(TOKENS + ROWS * owner, ROWS), ROWS), :]


def sum_kernel(parts_ref, kept_ref, come_ref, out_ref, send_ref, keep_ref):
    spread(parts_ref, out_ref)
    for k, ref in enumerate((keep_ref, send_ref)):
        ref[0] = kept_ref[k]
        ref[1] = come_ref[k]


def root_kernel(gram_ref, kept_ref, out_ref, product_ref):
    shards = [gram_ref[spot ^ SCATTER ^ GATHER] for spot in range(SHARDS)]
    packed = jnp.concatenate(shards, axis=0).astype(F32)
    take = lambda row, count: packed[row : row + count]
    pieces = {spot: take(LANES * piece, LANES) for piece, spot in enumerate(BELOW)}
    row = lax.broadcasted_iota(jnp.int32, (LANES, LANES), 0)
    column = lax.broadcasted_iota(jnp.int32, (LANES, LANES), 1)
    for pair in range(2):
        base = LANES * (len(BELOW) + pair)
        first = take(base, LANES)
        second = jnp.concatenate([take(base + HALF, HALF), take(LANES * (len(BELOW) + 2) + HALF * pair, HALF)], axis=0)
        pieces[2 * pair, 2 * pair] = jnp.where((row >= HALF) & (column < HALF), first.T, first)
        pieces[2 * pair + 1, 2 * pair + 1] = jnp.where((row < HALF) & (column >= HALF), second.T, second)
    entry = lambda row, column: pieces[row, column] if row >= column else pieces[column, row].T
    gram = jnp.concatenate(
        [jnp.concatenate([entry(row, column) for column in range(4)], axis=1) for row in range(4)], axis=0
    )
    row = lax.broadcasted_iota(jnp.int32, (B, B), 0)
    column = lax.broadcasted_iota(jnp.int32, (B, B), 1)
    identity = jnp.where(row == column, 1.0, 0.0).astype(F32)
    damped = gram * (1.0 / 65536) + DAMPING * identity
    norm = jnp.max(jnp.sum(jnp.abs(damped), axis=1, keepdims=True), axis=0, keepdims=True)
    dot = lambda left, right: jnp.dot(left, right, preferred_element_type=F32)
    y = damped * (1.0 / norm)
    near = y.astype(BF)
    square = dot(near, near)
    z = 2.25 * identity - 2.4375 * y + 1.6875 * square + dot(square.astype(BF), (0.0625 * square - 0.5625 * y).astype(BF))
    close = z.astype(BF)
    both = dot(jnp.concatenate([close, near], axis=0), close).astype(BF)
    root = 1.5 * z - 0.5 * dot(both[:B], both[B:])
    root = (root * (1.0 / jnp.sqrt(norm))).astype(BF)
    out_ref[...] = root
    product_ref[...] = dot(kept_ref[...].reshape(4 * ROWS, B), root).astype(BF)


def apply_kernel(root_ref, product_ref, come_ref, out_ref):
    spot = lax.axis_index("yh") ^ RETURN
    late = jnp.dot(come_ref[...].reshape(4 * ROWS, B), root_ref[...], preferred_element_type=F32).astype(BF)
    for product, flip in ((product_ref[...], 0), (late, SECOND)):
        for k in range(2):
            out_ref[spot ^ flip ^ (FIRST * k)] = product[2 * ROWS * k : 2 * ROWS * (k + 1)]


def local(activations, token_mask, gradient):
    mask = pltpu.with_memory_space_constraint(token_mask.reshape(1, TOKENS), pltpu.HBM)
    activations = pltpu.with_memory_space_constraint(activations, pltpu.HBM)
    gradient = pltpu.with_memory_space_constraint(gradient, pltpu.HBM)
    dma = pltpu.SemaphoreType.DMA
    (slab,) = call(
        slab_kernel,
        [((SLAB, B), BF)],
        (activations, mask, gradient),
        [HBM] * 3,
        [pltpu.VMEM((1, TOKENS), jnp.int32), dma((6,))],
    )
    other = lax.ppermute(slab, "core", [(0, 1), (1, 0)])
    own, mine = call(
        own_kernel,
        [((3, H, H), F32), ((4 * ROWS, B), BF)],
        (activations, mask, gradient),
        [HBM] * 3,
        [pltpu.VMEM((TOKENS, B), BF), pltpu.VMEM((1, TOKENS), jnp.int32), dma((6,))],
        flops=6 * TOKENS * H * H,
    )
    half = ((2, 2, ROWS, B), BF)
    (packed,) = call(gram_kernel, [((PIECES, LANES, LANES), BF)], (other, own), flops=6 * TOKENS * H * H)
    parts = lax.all_to_all(packed.reshape(SHARDS, PACKED, LANES), NAMES, 0, 0, axis_index_groups=planes(SCATTER))
    copies, send, kept = call(first_sum, [(parts.shape, BF), half, half], (parts, other, mine))
    come = lax.ppermute(send, NAMES, pairs(FIRST))
    parts = lax.all_to_all(copies, "z", 0, 0)
    copies, send, kept = call(sum_kernel, [(parts.shape, BF), half, half], (parts, kept, come))
    come = lax.ppermute(send, NAMES, pairs(SECOND))
    packed = lax.all_to_all(copies, NAMES, 0, 0, axis_index_groups=planes(GATHER))
    root, product = call(
        root_kernel, [((B, B), BF), ((4 * ROWS, B), BF)], (packed, kept), flops=2 * 5 * B * B * B
    )
    (product,) = call(
        apply_kernel, [((4, 2 * ROWS, B), BF)], (root, product, come), flops=2 * 4 * ROWS * B * B
    )
    product = lax.all_to_all(product.reshape(8, ROWS, B), NAMES, 0, 0, axis_index_groups=groups())
    product = jnp.concatenate([product[2 * (yh ^ RETURN) :][:2] for yh in range(4)], axis=0)
    return product.transpose(1, 0, 2).reshape(ROWS, 8 * B)


def solution(mesh):
    names, sizes = zip(*AXES)
    cut = Mesh(mesh.devices.reshape(sizes), names)
    dp = names[:4]
    placed = (P(dp, "yh"), P(dp), P(names, None))
    return jax.shard_map(local, mesh=cut, in_specs=placed, out_specs=P(names, None), check_vma=False)
```

```python
import jax
import jax.numpy as jnp
from jax import lax
from jax.experimental import pallas as pl
from jax.experimental.pallas import tpu as pltpu
from jax.sharding import Mesh, PartitionSpec as P

B = 512
H = 256
LANES = 128
DAMPING = 0.05
BF = jnp.bfloat16
F32 = jnp.float32
AXES = (("z", 8), ("yl", 2), ("x", 4), ("core", 2), ("yh", 4))
NAMES = tuple(name for name, _ in AXES)
SHARDS = 8
BELOW = [(row, column) for column in range(4) for row in range(column + 1, 4)]
PIECES = len(BELOW) + 3
PACKED = PIECES * LANES // SHARDS
HALF = LANES // 2
ROWS = 32
TOKENS = 512
MASK_ROWS = 16
SCATTER = 6
GATHER = 4
RETURN = 2
FIRST = 3
SECOND = 1
SLAB = TOKENS + 4 * ROWS + MASK_ROWS
VMEM_MIB = 16
VMEM = pl.BlockSpec(memory_space=pltpu.VMEM)
HBM = pl.BlockSpec(memory_space=pltpu.HBM)


def place(z, yl, x, core, yh):
    return (((z * 2 + yl) * 4 + x) * 2 + core) * 4 + yh


def groups():
    orders = [k ^ RETURN for k in range(4)]
    every = [(z, w, x) for z in range(8) for w in range(2) for x in range(4)]
    return [[place(z, w ^ (yh >> 1), x, core, yh) for yh in orders for core in range(2)] for z, w, x in every]


def planes(first):
    spots = [divmod(k ^ first, 4) for k in range(SHARDS)]
    return [[place(z, yl, x, core, yh) for yl, x in spots] for z in range(8) for core in range(2) for yh in range(4)]


def pairs(flip):
    ends = [(2 * yh + core, 2 * (yh ^ flip) + core) for yh in range(4) for core in range(2)]
    return [(group[source], group[target]) for group in groups() for source, target in ends]


def call(kernel, outs, operands, specs=None, scratch=(), flops=0):
    shapes = [jax.ShapeDtypeStruct(*out) for out in outs]
    moved = sum(o.size * o.dtype.itemsize for o in (*operands, *shapes))
    return pl.pallas_call(
        kernel,
        out_shape=shapes,
        in_specs=specs or [VMEM] * len(operands),
        out_specs=[VMEM] * len(outs),
        scratch_shapes=scratch,
        cost_estimate=pl.CostEstimate(flops=flops, bytes_accessed=moved, transcendentals=0),
        compiler_params=pltpu.CompilerParams(vmem_limit_bytes=VMEM_MIB * 1024 * 1024),
    )(*operands)


def at(index, size=B):
    return pl.ds(pl.multiple_of(index * size, size), size)


def slab_kernel(act_ref, mask_ref, grad_ref, out_ref, mask_held, sems):
    other = 1 - lax.axis_index("core")
    copies = [pltpu.make_async_copy(act_ref.at[:, at(other)], out_ref.at[pl.ds(0, TOKENS)], sems.at[0])]
    for k in range(4):
        rows = pl.ds(TOKENS + ROWS * k, ROWS)
        copies.append(pltpu.make_async_copy(grad_ref.at[:, at(2 * k + other)], out_ref.at[rows], sems.at[k + 1]))
    copies.insert(1, pltpu.make_async_copy(mask_ref, mask_held, sems.at[5]))
    for copy in copies:
        copy.start()
    copies.pop(1).wait()
    mask = mask_held[...].astype(F32).astype(BF)
    out_ref[pl.ds(TOKENS + 4 * ROWS, MASK_ROWS), :] = jnp.broadcast_to(mask, (MASK_ROWS, TOKENS))
    for copy in copies:
        copy.wait()


def masked(columns, mask):
    column = jnp.broadcast_to(mask.astype(F32), (LANES, TOKENS)).T.astype(BF)
    return columns * jnp.concatenate([column] * (B // LANES), axis=1)


def triangle(columns):
    dot = lambda a, b: lax.dot_general(a, b, (((0,), (0,)), ((), ())), preferred_element_type=F32)
    low, high = columns[:, :H], columns[:, H:]
    return dot(low, low), dot(high, low), dot(high, high)


def own_kernel(act_ref, mask_ref, grad_ref, out_ref, mine_ref, held, mask_held, sems):
    core = lax.axis_index("core")
    copies = [pltpu.make_async_copy(act_ref.at[:, at(core)], held, sems.at[0])]
    copies.append(pltpu.make_async_copy(mask_ref, mask_held, sems.at[1]))
    for k in range(4):
        rows = pl.ds(ROWS * k, ROWS)
        copies.append(pltpu.make_async_copy(grad_ref.at[:, at(2 * k + core)], mine_ref.at[rows], sems.at[k + 2]))
    for copy in copies:
        copy.start()
    for copy in copies:
        copy.wait()
    for slot, block in enumerate(triangle(masked(held[...], mask_held[...]))):
        out_ref[slot] = block


def gram_kernel(slab_ref, own_ref, out_ref):
    mask = slab_ref[pl.ds(TOKENS + 4 * ROWS, MASK_ROWS), :][:1]
    blocks = triangle(masked(slab_ref[pl.ds(0, TOKENS), :], mask))
    blocks = [block + own_ref[slot] for slot, block in enumerate(blocks)]
    def cut(row, column):
        block = blocks[row // 2 + column // 2]
        row, column = LANES * (row % 2), LANES * (column % 2)
        return block[row : row + LANES, column : column + LANES]

    for piece, spot in enumerate(BELOW):
        out_ref[piece] = cut(*spot).astype(BF)
    left = lax.broadcasted_iota(jnp.int32, (HALF, LANES), 1) < HALF
    for pair in range(2):
        first, second = cut(2 * pair, 2 * pair), cut(2 * pair + 1, 2 * pair + 1)
        shared = jnp.where(left, second[:HALF], first[HALF:])
        out_ref[len(BELOW) + pair] = jnp.concatenate([first[:HALF], shared], axis=0).astype(BF)
        out_ref[len(BELOW) + 2, pl.ds(HALF * pair, HALF)] = second[HALF:].astype(BF)


def spread(parts_ref, out_ref):
    total = parts_ref[0].astype(F32)
    for part in range(1, SHARDS):
        total += parts_ref[part].astype(F32)
    rounded = total.astype(BF)
    for copy in range(SHARDS):
        out_ref[copy] = rounded


def first_sum(parts_ref, slab_ref, mine_ref, out_ref, send_ref, keep_ref):
    spread(parts_ref, out_ref)
    core, tensor = lax.axis_index("core"), lax.axis_index("yh")
    for ref, flip in ((send_ref, FIRST), (keep_ref, 0)):
        for k in range(2):
            owner = tensor ^ flip ^ (SECOND * k)
            ref[k, core] = mine_ref[at(owner, ROWS), :]
            ref[k, 1 - core] = slab_ref[pl.ds(pl.multiple_of(TOKENS + ROWS * owner, ROWS), ROWS), :]


def sum_kernel(parts_ref, kept_ref, come_ref, out_ref, send_ref, keep_ref):
    spread(parts_ref, out_ref)
    for k, ref in enumerate((keep_ref, send_ref)):
        ref[0] = kept_ref[k]
        ref[1] = come_ref[k]


def root_kernel(gram_ref, kept_ref, out_ref, product_ref):
    shards = [gram_ref[spot ^ SCATTER ^ GATHER] for spot in range(SHARDS)]
    packed = jnp.concatenate(shards, axis=0).astype(F32)
    take = lambda row, count: packed[row : row + count]
    pieces = {spot: take(LANES * piece, LANES) for piece, spot in enumerate(BELOW)}
    row = lax.broadcasted_iota(jnp.int32, (LANES, LANES), 0)
    column = lax.broadcasted_iota(jnp.int32, (LANES, LANES), 1)
    for pair in range(2):
        base = LANES * (len(BELOW) + pair)
        first = take(base, LANES)
        second = jnp.concatenate([take(base + HALF, HALF), take(LANES * (len(BELOW) + 2) + HALF * pair, HALF)], axis=0)
        pieces[2 * pair, 2 * pair] = jnp.where((row >= HALF) & (column < HALF), first.T, first)
        pieces[2 * pair + 1, 2 * pair + 1] = jnp.where((row < HALF) & (column >= HALF), second.T, second)
    entry = lambda row, column: pieces[row, column] if row >= column else pieces[column, row].T
    gram = jnp.concatenate(
        [jnp.concatenate([entry(row, column) for column in range(4)], axis=1) for row in range(4)], axis=0
    )
    row = lax.broadcasted_iota(jnp.int32, (B, B), 0)
    column = lax.broadcasted_iota(jnp.int32, (B, B), 1)
    identity = jnp.where(row == column, 1.0, 0.0).astype(F32)
    damped = gram * (1.0 / 65536) + DAMPING * identity
    norm = jnp.max(jnp.sum(jnp.abs(damped), axis=1, keepdims=True), axis=0, keepdims=True)
    dot = lambda left, right: jnp.dot(left, right, preferred_element_type=F32)
    y = damped * (1.0 / norm)
    near = y.astype(BF)
    square = dot(near, near)
    z = 2.25 * identity - 2.4375 * y + 1.6875 * square + dot(square.astype(BF), (0.0625 * square - 0.5625 * y).astype(BF))
    close = z.astype(BF)
    both = dot(jnp.concatenate([close, near], axis=0), close).astype(BF)
    root = 1.5 * z - 0.5 * dot(both[:B], both[B:])
    root = (root * (1.0 / jnp.sqrt(norm))).astype(BF)
    out_ref[...] = root
    product_ref[...] = dot(kept_ref[...].reshape(4 * ROWS, B), root).astype(BF)


def apply_kernel(root_ref, product_ref, come_ref, out_ref):
    spot = lax.axis_index("yh") ^ RETURN
    late = jnp.dot(come_ref[...].reshape(4 * ROWS, B), root_ref[...], preferred_element_type=F32).astype(BF)
    for product, flip in ((product_ref[...], 0), (late, SECOND)):
        for k in range(2):
            out_ref[spot ^ flip ^ (FIRST * k)] = product[2 * ROWS * k : 2 * ROWS * (k + 1)]


def local(activations, token_mask, gradient):
    mask = pltpu.with_memory_space_constraint(token_mask.reshape(1, TOKENS), pltpu.HBM)
    activations = pltpu.with_memory_space_constraint(activations, pltpu.HBM)
    gradient = pltpu.with_memory_space_constraint(gradient, pltpu.HBM)
    dma = pltpu.SemaphoreType.DMA
    (slab,) = call(
        slab_kernel,
        [((SLAB, B), BF)],
        (activations, mask, gradient),
        [HBM] * 3,
        [pltpu.VMEM((1, TOKENS), jnp.int32), dma((6,))],
    )
    other = lax.ppermute(slab, "core", [(0, 1), (1, 0)])
    own, mine = call(
        own_kernel,
        [((3, H, H), F32), ((4 * ROWS, B), BF)],
        (activations, mask, gradient),
        [HBM] * 3,
        [pltpu.VMEM((TOKENS, B), BF), pltpu.VMEM((1, TOKENS), jnp.int32), dma((6,))],
        flops=6 * TOKENS * H * H,
    )
    half = ((2, 2, ROWS, B), BF)
    (packed,) = call(gram_kernel, [((PIECES, LANES, LANES), BF)], (other, own), flops=6 * TOKENS * H * H)
    parts = lax.all_to_all(packed.reshape(SHARDS, PACKED, LANES), NAMES, 0, 0, axis_index_groups=planes(SCATTER))
    copies, send, kept = call(first_sum, [(parts.shape, BF), half, half], (parts, other, mine))
    come = lax.ppermute(send, NAMES, pairs(FIRST))
    parts = lax.all_to_all(copies, "z", 0, 0)
    copies, send, kept = call(sum_kernel, [(parts.shape, BF), half, half], (parts, kept, come))
    come = lax.ppermute(send, NAMES, pairs(SECOND))
    packed = lax.all_to_all(copies, NAMES, 0, 0, axis_index_groups=planes(GATHER))
    root, product = call(
        root_kernel, [((B, B), BF), ((4 * ROWS, B), BF)], (packed, kept), flops=2 * 5 * B * B * B
    )
    (product,) = call(
        apply_kernel, [((4, 2 * ROWS, B), BF)], (root, product, come), flops=2 * 4 * ROWS * B * B
    )
    product = lax.all_to_all(product.reshape(8, ROWS, B), NAMES, 0, 0, axis_index_groups=groups())
    product = jnp.concatenate([product[2 * (yh ^ RETURN) :][:2] for yh in range(4)], axis=0)
    return product.transpose(1, 0, 2).reshape(ROWS, 8 * B)


def solution(mesh):
    names, sizes = zip(*AXES)
    cut = Mesh(mesh.devices.reshape(sizes), names)
    dp = names[:4]
    placed = (P(dp, "yh"), P(dp), P(names, None))
    return jax.shard_map(local, mesh=cut, in_specs=placed, out_specs=P(names, None), check_vma=False)
```
